256 devices in a mesh: dp: 64 (over z, y_hi, x), ctx: 4 (over y_lo, core).
Axes of the slice: x: 4, y: 4 (y_hi: 2, y_lo: 2; y = y_hi * 2 + y_lo), z: 8, core: 2. Of those that a mesh axis runs over, the one named last changes fastest.
Arguments:
- gated_hidden_input: bfloat16 [64, 2, 256, 29568], P('dp', None, 'ctx'), may hold values from -16 to 16
- frozen: bfloat16 [64, 2, 256, 8192], P('dp', None, 'ctx'), may hold values from -25 to 25
- head_gradient_rows: bfloat16 [64, 2, 256, 8192], P('dp', None, 'ctx'), may hold values from -0.875 to 0.875
- down_factor_weight: bfloat16 [29568, 64], P('dp'), may hold values from -0.03125 to 0.03125
- up_factor_weight: bfloat16 [64, 8192], P(None, 'dp'), may hold values from -0.1875 to 0.1875
- final_norm_gain: bfloat16 [8192], P('dp'), may hold values from 0.5 to 1.5
- logratio: float32 [64, 2, 256], P('dp', None, 'ctx'), may hold values from -8 to 8
- starts: int32 [64, 2], P('dp'), may hold values from 0 to 127
Outputs:
- preference_pair_loss: float32 [64], P('dp')
- gradient_down_factor: float32 [29568, 64], P('dp')
- gradient_up_factor: float32 [64, 8192], P(None, 'dp')
The draws below stay inside these ranges and needn't reach their ends.
All inputs are finite; a program needn't handle non-finite values.
Results may differ from the reference program's by a relative error of at most 0.007.
Values may be sent and summed in bfloat16 or wider, within the bound.
No kernel may reach another device: no remote copies, remote signals or barrier semaphores. Data moves between devices by JAX's collectives and lax.ppermute only.
A program may use at most 128 MiB of HBM per device.

```python
import jax
import jax.numpy as jnp
from jax import lax

MODEL_DIM = 8192
FEEDFWD_UNITS = 29568
ADAPTER_ORDER = 64
SEQ = 256
PAIRS = 64


def draw_frozen(key, part):
    key = jax.random.fold_in(key, 3)
    subkeys = jax.random.split(key, 1)
    full_shape = (PAIRS, 2, SEQ, MODEL_DIM)
    values = jnp.clip(jax.random.normal(subkeys[0], full_shape, jnp.float32), -6.0, 6.0)
    return values.astype(jnp.bfloat16)


def draw_logratio(key, part):
    key = jax.random.fold_in(key, 5)
    full_shape = (PAIRS, 2, SEQ)
    ramp = 0.25 + jnp.arange(SEQ).astype(jnp.float32) / SEQ
    noise = jnp.clip(jax.random.normal(key, full_shape, jnp.float32), -6.0, 6.0)
    values = noise * ramp[None, None, :]
    return values


def set_ends(values, own_key, low, high):
    longest = values.shape.index(max(values.shape))
    spots = []
    for shift in (0, 1):
        where = [jax.random.randint(jax.random.fold_in(own_key, axis), (), 0, length) for axis, length in enumerate(values.shape)]
        where[longest] = (where[longest] + shift) % values.shape[longest]
        spots.append(tuple(where))
    return values.at[spots[0]].set(low).at[spots[1]].set(high)


def spiked(result, rng, source, target, shards_of, factor):
    def block_of(dim):
        return (jnp.arange(result.shape[dim]) // (result.shape[dim] // shards_of)).reshape((-1,) + (1,) * (result.ndim - 1 - dim))

    one_side = jax.random.permutation(rng, shards_of)[block_of(target)]
    other_side = (block_of(target) + shards_of // 2) % shards_of
    return jnp.where((block_of(source) == one_side) | (block_of(source) == other_side), factor * result, result)


def steps_of(rng, shape, shards, low, largest):
    gain, own = 1.0, jax.random.fold_in(rng, 6)
    for dim, blocks in shards:
        steps = jnp.exp(jax.random.uniform(jax.random.fold_in(own, dim), (blocks,), jnp.float32, low / len(shards), largest / len(shards)))
        gain = gain * jnp.repeat(steps, shape[dim] // blocks).reshape([-1 if axis == dim else 1 for axis in range(len(shape))])
    return gain


def scatter_about(key, shape, deviation, bound, pieces=(), held_as=jnp.bfloat16):
    result = jax.random.normal(key, shape, jnp.float32) * deviation
    if len(pieces) > 0:
        result = steps_of(key, shape, pieces, -0.22, 0.18) * result
    return jnp.clip(result, min=-bound, max=bound).astype(held_as)


def bell_draw_with(rng, extent, deviation, limit, pieces, heavy, kind=jnp.bfloat16):
    drawn = deviation * jax.random.normal(rng, extent, jnp.float32)
    if pieces:
        drawn = drawn * steps_of(rng, extent, pieces, -0.22, 0.18)
    return jnp.clip(spiked(drawn, jax.random.fold_in(rng, 3), *heavy), -limit, limit).astype(kind)


def setup_inputs(seed: int = 0) -> dict:
    keys = jax.random.split(jax.random.key(seed), 9)
    gated_hidden_input = bell_draw_with(keys[0], (PAIRS, 2, SEQ, FEEDFWD_UNITS), 1.0, 16.0, ((0, 64), (2, 4)), (0, 3, 64, 4.0))
    frozen = draw_frozen(jax.random.fold_in(keys[8], 71), 0)
    head_gradient_rows = bell_draw_with(keys[2], (PAIRS, 2, SEQ, MODEL_DIM), 0.05, 0.875, ((0, 64), (2, 4)), (0, 3, 64, 4.0))
    down_factor_weight = scatter_about(keys[3], (FEEDFWD_UNITS, ADAPTER_ORDER), FEEDFWD_UNITS ** -0.5, 0.03125, ((0, 64),))
    up_factor_weight = scatter_about(keys[4], (ADAPTER_ORDER, MODEL_DIM), (ADAPTER_ORDER * 16) ** -0.5, 0.1875, ((1, 64),))
    final_norm_gain = jnp.clip(1.0 + 0.1 * jax.random.normal(keys[5], (MODEL_DIM,), jnp.float32), 0.5, 1.5).astype(jnp.bfloat16)
    logratio = draw_logratio(jax.random.fold_in(keys[8], 71), 0)
    starts = set_ends(jax.random.randint(keys[7], (PAIRS, 2), 0, SEQ // 2), jax.random.fold_in(keys[7], 1), 0, (SEQ // 2) - 1).astype(jnp.int32)
    return dict(gated_hidden_input=gated_hidden_input, frozen=frozen, head_gradient_rows=head_gradient_rows, down_factor_weight=down_factor_weight, up_factor_weight=up_factor_weight, final_norm_gain=final_norm_gain, logratio=logratio, starts=starts)


ADAPTER_SCALING = 2.0
DPO_BETA = 0.1
NORM_EPSILON = 1e-06

def reference(gated_hidden_input, frozen, head_gradient_rows, down_factor_weight, up_factor_weight, final_norm_gain, logratio, starts):
    precise_result = lax.Precision.HIGHEST
    positions = jnp.arange(SEQ).astype(jnp.int32)
    keep_mask = (positions[None, None, :] >= starts[:, :, None]).astype(jnp.float32)
    seq_sum = lax.optimization_barrier(jnp.sum(keep_mask * logratio, axis=2))
    margin = DPO_BETA * (seq_sum[:, 0] - seq_sum[:, 1])
    preference_pair_loss = jnp.logaddexp(0.0, -margin)
    sides = jnp.array([1.0, -1.0], jnp.float32)
    row_gradient_slope = (-DPO_BETA * jax.nn.sigmoid(-margin))[:, None, None] * sides[None, :, None] * keep_mask
    gain_f32 = final_norm_gain.astype(jnp.float32)
    up_single_float = up_factor_weight.astype(jnp.float32)

    def single_pair_loss(carry, inputs):
        hidden, resid, upstream, slope = inputs
        hidden_row_block = hidden.reshape(-1, FEEDFWD_UNITS)
        residual_row_block = resid.reshape(-1, MODEL_DIM).astype(jnp.float32)
        adapter_bfloat_copy = jnp.dot(hidden_row_block, down_factor_weight, preferred_element_type=jnp.float32).astype(jnp.bfloat16)
        adapter_single_float = adapter_bfloat_copy.astype(jnp.float32)
        policy_hidden_state = residual_row_block + ADAPTER_SCALING * jnp.dot(adapter_bfloat_copy, up_factor_weight, preferred_element_type=jnp.float32)
        policy_rms = jnp.sqrt(lax.optimization_barrier(jnp.mean(policy_hidden_state * policy_hidden_state, axis=1)) + NORM_EPSILON)
        gained = slope.reshape(-1)[:, None] * upstream.reshape(-1, MODEL_DIM).astype(jnp.float32) * gain_f32[None, :]
        inner = lax.optimization_barrier(jnp.sum(gained * policy_hidden_state, axis=1))
        gradient_state_rows = gained / policy_rms[:, None] - policy_hidden_state * (inner / (MODEL_DIM * policy_rms * policy_rms * policy_rms))[:, None]
        gradient_reduced_precision = ADAPTER_SCALING * jnp.dot(gradient_state_rows, up_single_float.T, precision=precise_result)
        down_acc, up_accumulator = carry
        down_acc = down_acc + jnp.dot(hidden_row_block.astype(jnp.float32).T, gradient_reduced_precision, precision=precise_result)
        up_accumulator = up_accumulator + ADAPTER_SCALING * jnp.dot(adapter_single_float.T, gradient_state_rows, precision=precise_result)
        return ((down_acc, up_accumulator), None)
    initial_hidden_state = (jnp.zeros((FEEDFWD_UNITS, ADAPTER_ORDER), jnp.float32), jnp.zeros((ADAPTER_ORDER, MODEL_DIM), jnp.float32))
    (gradient_down_factor, gradient_up_factor), unused_item = lax.scan(single_pair_loss, initial_hidden_state, (gated_hidden_input, frozen, head_gradient_rows, row_gradient_slope))
    return (preference_pair_loss, gradient_down_factor, gradient_up_factor)
```

```python
import jax
import jax.numpy as jnp
from jax import lax
from jax.sharding import Mesh, PartitionSpec as P

ADAPTER_SCALING = 2.0
DPO_BETA = 0.1
NORM_EPSILON = 1e-06

FINE_AXES = ("z", "yh", "x", "yl", "c")
FINE_SHAPE = (8, 2, 4, 2, 2)
DP = ("z", "yh", "x")
CTX = ("yl", "c")
LANES = 640


def spread(values, axes, count):
    copies = jnp.broadcast_to(values[None], (count,) + values.shape)
    return lax.all_to_all(copies, axes, 0, 0, tiled=True)


def exchange_sum(values, axes):
    moved = lax.all_to_all(values, axes, 0, 0, tiled=True)
    return jnp.sum(moved.astype(jnp.float32), axis=0)


def token_contract(values, left_rows):
    upper_part = values.astype(jnp.bfloat16)
    return jnp.einsum("tk,tf->kf", upper_part, left_rows, preferred_element_type=jnp.float32)


def local(
    gated_hidden_input,
    frozen,
    head_gradient_rows,
    down_factor_weight,
    up_factor_weight,
    final_norm_gain,
    logratio,
    starts,
):
    row_block = frozen.shape[2]
    model_width = frozen.shape[3]
    own_hidden = gated_hidden_input.reshape(-1, gated_hidden_input.shape[3])
    down_rows, order = down_factor_weight.shape
    up_columns = up_factor_weight.shape[1]
    used = down_rows + up_columns
    yl, core = lax.axis_index("yl"), lax.axis_index("c")

    gain_columns = final_norm_gain.reshape(-1, order).T
    block = jnp.concatenate([down_factor_weight.T, up_factor_weight, gain_columns], axis=1)
    block = jnp.pad(block, ((0, 0), (0, LANES - block.shape[1])))
    quarter = lax.dynamic_slice_in_dim(block, core * 32 + yl * 16, 16, axis=0)
    held = spread(quarter, "z", 8)
    held = spread(held, ("yh", "yl"), 4)
    held = spread(held, "x", 4)
    held = spread(held, "c", 2)
    held = held.reshape(2, 4, 2, 2, 8, 16, LANES).transpose(0, 3, 5, 4, 2, 1, 6)
    held = held.reshape(order, 64, LANES)
    down_t = held[:, :, :down_rows].reshape(order, -1)
    up_full = held[:, :, down_rows:used].reshape(order, -1)
    gain_full = held[:, :, used : used + gain_columns.shape[1]].transpose(1, 2, 0).reshape(-1)
    gain_f32 = gain_full.astype(jnp.float32)

    position_shape = (1, 1, row_block)
    positions = (yl * 2 + core) * row_block + lax.broadcasted_iota(jnp.int32, position_shape, 2)
    keep_mask = (positions >= starts[:, :, None]).astype(jnp.float32)
    seq_sum = lax.psum(jnp.sum(keep_mask * logratio, axis=2), CTX)
    margin = DPO_BETA * (seq_sum[:, 0] - seq_sum[:, 1])
    preference_pair_loss = jnp.logaddexp(0.0, -margin)
    sides = jnp.array([1.0, -1.0], jnp.float32)
    row_gradient_slope = (
        (-DPO_BETA * jax.nn.sigmoid(-margin))[:, None, None] * sides[None, :, None] * keep_mask
    ).reshape(-1)

    adapter_bfloat_copy = jnp.einsum(
        "tf,kf->tk", own_hidden, down_t, preferred_element_type=jnp.float32
    ).astype(jnp.bfloat16)
    residual_row_block = frozen.reshape(-1, model_width).astype(jnp.float32)
    policy_hidden_state = residual_row_block + ADAPTER_SCALING * jnp.dot(
        adapter_bfloat_copy, up_full, preferred_element_type=jnp.float32
    )
    policy_rms = jnp.sqrt(
        jnp.mean(policy_hidden_state * policy_hidden_state, axis=1) + NORM_EPSILON
    )
    gained = (
        row_gradient_slope[:, None]
        * head_gradient_rows.reshape(-1, model_width).astype(jnp.float32)
        * gain_f32[None, :]
    )
    inner = jnp.sum(gained * policy_hidden_state, axis=1)
    gradient_state_rows = (
        gained / policy_rms[:, None]
        - policy_hidden_state
        * (inner / (model_width * policy_rms * policy_rms * policy_rms))[:, None]
    )
    gradient_low = ADAPTER_SCALING * lax.dot_general(
        gradient_state_rows,
        up_full.astype(jnp.float32),
        (((1,), (1,)), ((), ())),
        precision=lax.Precision.HIGHEST,
    )
    down_gradient = token_contract(gradient_low, own_hidden)
    up_gradient = ADAPTER_SCALING * jnp.einsum(
        "tk,td->kd",
        adapter_bfloat_copy,
        gradient_state_rows.astype(jnp.bfloat16),
        preferred_element_type=jnp.float32,
    )
    packed = jnp.concatenate(
        [
            down_gradient.reshape(order, 64, down_rows).astype(jnp.bfloat16),
            up_gradient.reshape(order, 64, up_columns).astype(jnp.bfloat16),
        ],
        axis=2,
    )
    packed = jnp.pad(packed, ((0, 0), (0, 0), (0, LANES - used)))
    packed = packed.reshape(2, 2, 16, 8, 2, 4, LANES).transpose(0, 5, 3, 4, 1, 2, 6)
    share = exchange_sum(packed, "c").astype(jnp.bfloat16)
    share = exchange_sum(share, "x").astype(jnp.bfloat16)
    share = share.reshape(32, 16, LANES)
    share = exchange_sum(share, ("z", "yh", "yl"))
    whole = spread(share, CTX, 4).reshape(2, 2, 16, LANES).transpose(1, 0, 2, 3)
    whole = whole.reshape(order, LANES)
    return (
        preference_pair_loss,
        whole[:, :down_rows].T,
        whole[:, down_rows:used],
    )


def solution(mesh):
    fine = Mesh(mesh.devices.reshape(FINE_SHAPE), FINE_AXES)
    return jax.shard_map(
        local,
        mesh=fine,
        in_specs=(
            P(DP, None, CTX, None),
            P(DP, None, CTX, None),
            P(DP, None, CTX, None),
            P(DP, None),
            P(None, DP),
            P(DP),
            P(DP, None, CTX),
            P(DP, None),
        ),
        out_specs=(P(DP), P(DP, None), P(None, DP)),
        check_vma=False,
    )
```

```python
import jax
import jax.numpy as jnp
from jax import lax
from jax.experimental import pallas as pl
from jax.experimental.pallas import tpu as pltpu
from jax.sharding import Mesh, PartitionSpec as P

SCALE = 2.0
BETA = 0.1
EPS = 1e-06

FINE_AXES = ("z", "yh", "x", "yl", "c")
FINE_SHAPE = (8, 2, 4, 2, 2)
DP = ("z", "yh", "x")
CTX = ("yl", "c")
Y = ("yh", "yl")

LANES = 640
UP = 128
DOWN = 462
GAIN_AT = UP + DOWN
SUMS_AT = GAIN_AT + 32
CHUNKS = 64
ORDER = 64
BF, F32 = jnp.bfloat16, jnp.float32
NT = (((1,), (1,)), ((), ()))
NN = (((1,), (0,)), ((), ()))


def dot(a, b, dims):
    return lax.dot_general(a, b, dims, preferred_element_type=F32)


def slots(place, sign):
    py, px, pc = place[1], place[2], place[3]
    dxs = [(sign * (px - x)) & 3 for x in range(4)]
    dys = [(sign * (py - y)) & 3 for y in range(4)]
    cores = [((pc + c) & 1) * 128 for c in range(2)]

    def flat(chunk, q):
        z, yh, x = chunk // 8, chunk // 4 % 2, chunk % 4
        c, y = q // 2, yh * 2 + q % 2
        if z < 4:
            return cores[c] + dys[y] * 4 + (x * 16 + z)
        return cores[c] + dys[y] * 16 + dxs[x] * 4 + (60 + z)

    return flat


def kernel(place_ref, starts_ref, *refs):
    parts, (hidden_hbm, frozen_hbm, head_hbm) = refs[:10], refs[10:13]
    outs, margin_ref = refs[13:23], refs[23]
    hid, fro, hea, wt, up, gains, gain, pol, block, sems = refs[24:]
    width = fro.shape[1]

    def ranges():
        begin = 0
        for i in range(10):
            size = 64 if i % 5 == 0 else 16
            yield pl.ds(begin, size)
            begin += size

    loads = [
        pltpu.make_async_copy(parts[i], block.at[at], sems.at[i]) for i, at in enumerate(ranges())
    ]
    loads.append(pltpu.make_async_copy(hidden_hbm, hid, sems.at[10]))
    loads.append(pltpu.make_async_copy(frozen_hbm, fro, sems.at[11]))
    loads.append(pltpu.make_async_copy(head_hbm, hea, sems.at[12]))
    for copy in loads:
        copy.start()
    for copy in loads[:10]:
        copy.wait()

    pz, py, px, pc = (place_ref[i] for i in range(4))
    sums = jnp.zeros((1, 128), F32)
    for c in range(2):
        for yl in range(2):
            dy = (py - ((py & 2) + yl)) & 3
            inside = jnp.where(pz < 4, px * 16 + dy * 4 + pz, 60 + dy * 16 + pz)
            held = block[((pc + c) & 1) * 128 + inside]
            sums += held[0:1, LANES - 128 :].astype(F32)
    lane = SUMS_AT - (LANES - 128)
    sides = [sum(sums[:, lane + 3 * s + j : lane + 3 * s + j + 1] for j in range(3)) for s in (0, 1)]
    margin = BETA * (sides[0] - sides[1])
    margin_ref[...] = jnp.broadcast_to(margin, margin_ref.shape)
    row = lax.broadcasted_iota(jnp.int32, (128, 1), 0)
    position = (row & 63) + ((py & 1) * 2 + pc) * 64
    start = jnp.where(row < 64, starts_ref[0, 0], starts_ref[0, 1])
    weight = jnp.where(row < 64, -BETA, BETA)
    slope = jnp.where(position >= start, weight, 0.0) / (1.0 + jnp.exp(margin))

    source = slots(place_ref, 1)
    for chunk in range(CHUNKS):
        for q in range(4):
            held = block[source(chunk, q)]
            rows = slice(16 * q, 16 * q + 16)
            up[rows, chunk * UP : (chunk + 1) * UP] = held[:, :UP]
            wt[rows, chunk * DOWN : (chunk + 1) * DOWN] = held[:, UP : UP + DOWN]
            gains[q, chunk : chunk + 1, :] = held[0:1, LANES - 128 :].astype(F32)
    lane = GAIN_AT - (LANES - 128)
    gain[...] = jnp.concatenate([gains[q][:, lane : lane + 32] for q in range(4)], axis=1)

    loads[10].wait()
    tile = 2688

    def low_step(i, total):
        at = pl.ds(pl.multiple_of(i * tile, 128), tile)
        return total + dot(hid[:, at], wt[:, at], NT)

    low = lax.fori_loop(0, wt.shape[1] // tile, low_step, jnp.zeros((128, ORDER), F32)).astype(BF)
    low_t = low.astype(F32).T.astype(BF)

    loads[11].wait()
    loads[12].wait()
    step = 512

    def gained(i):
        pieces = []
        for j in range(step // 128):
            at = pl.ds(pl.multiple_of(i * step + j * 128, 128), 128)
            pieces.append(hea[:, at].astype(F32) * gain[pl.ds(i * (step // 128) + j, 1), :])
        return jnp.concatenate(pieces, axis=1)

    def fold(v):
        return sum(v[:, 128 * j : 128 * j + 128] for j in range(step // 128))

    def state_step(i, carry):
        squares, inner = carry
        at = pl.ds(pl.multiple_of(i * step, 128), step)
        state = fro[:, at].astype(F32) + SCALE * dot(low, up[:, at], NN)
        pol[:, at] = state
        return squares + fold(state * state), inner + fold(gained(i) * state)

    zero = jnp.zeros((128, 128), F32)
    squares, inner = lax.fori_loop(0, width // step, state_step, (zero, zero))
    rms = jnp.sqrt(jnp.sum(squares, axis=1, keepdims=True) / width + EPS)
    inner = slope * jnp.sum(inner, axis=1, keepdims=True)
    first = slope / rms
    second = inner / (width * rms * rms * rms)

    target = slots(place_ref, -1)
    total = jnp.zeros((128, ORDER), F32)
    for i in range(width // step):
        at = slice(i * step, (i + 1) * step)
        grad = gained(i) * first - pol[:, at] * second
        high = grad.astype(BF)
        rest = (grad - high.astype(F32)).astype(BF)
        total += dot(high, up[:, at], NT) + dot(rest, up[:, at], NT)
        share = (SCALE * dot(low_t, high, NN)).astype(BF)
        for j in range(step // 128):
            for q in range(4):
                block[target(i * (step // 128) + j, q), :, :UP] = share[
                    16 * q : 16 * q + 16, 128 * j : 128 * j + 128
                ]
    grad_low = (SCALE * total).T.astype(BF)

    for chunk in range(CHUNKS):
        begin = chunk * DOWN // 128 * 128
        shift = chunk * DOWN - begin
        span = 512 if shift + DOWN <= 512 else 640
        share = dot(grad_low, hid[:, begin : begin + span], NN)
        if shift:
            share = pltpu.roll(share, span - shift, 1)
        share = share[:, :512].astype(BF)
        for q in range(4):
            block[target(chunk, q), :, UP:] = share[16 * q : 16 * q + 16]

    stores = [
        pltpu.make_async_copy(block.at[at], outs[i], sems.at[i]) for i, at in enumerate(ranges())
    ]
    for copy in stores:
        copy.start()
    for copy in stores:
        copy.wait()


def shares(place, starts, parts, hidden, frozen, head):
    rows, units = hidden.shape
    width = frozen.shape[1]
    any_space = pl.BlockSpec(memory_space=pl.ANY)
    smem = pl.BlockSpec(memory_space=pltpu.SMEM)
    sizes = ([64] + [16] * 4) * 2
    outs = pl.pallas_call(
        kernel,
        out_shape=[jax.ShapeDtypeStruct((n, 16, LANES), BF) for n in sizes]
        + [jax.ShapeDtypeStruct((8, 128), F32)],
        in_specs=[smem, smem] + [any_space] * 13,
        out_specs=[any_space] * 10 + [pl.BlockSpec(memory_space=pltpu.VMEM)],
        scratch_shapes=[
            pltpu.VMEM((rows, units), BF),
            pltpu.VMEM((rows, width), BF),
            pltpu.VMEM((rows, width), BF),
            pltpu.VMEM((ORDER, units), BF),
            pltpu.VMEM((ORDER, width), BF),
            pltpu.VMEM((4, CHUNKS, 128), F32),
            pltpu.VMEM((CHUNKS, 128), F32),
            pltpu.VMEM((rows, width), F32),
            pltpu.VMEM((256, 16, LANES), BF),
            pltpu.SemaphoreType.DMA((13,)),
        ],
        compiler_params=pltpu.CompilerParams(vmem_limit_bytes=40 * 1024 * 1024),
        cost_estimate=pl.CostEstimate(
            flops=2 * rows * ORDER * (2 * units + 4 * width),
            bytes_accessed=2 * rows * (units + 2 * width) + 4 * 256 * 16 * LANES,
            transcendentals=0,
        ),
    )(place, starts, *parts, hidden, frozen, head)
    return outs[:5], outs[5:10], outs[10][0, 0:1]


def ring(values, axes, count, step):
    return lax.ppermute(values, axes, [(i, (i + step) % count) for i in range(count)])


def spread(values, axes, count):
    copies = jnp.broadcast_to(values[None], (count,) + values.shape)
    return lax.all_to_all(copies, axes, 0, 0, tiled=True)


def together(*values):
    return lax.optimization_barrier(tuple(values))


def total_of(*values):
    return sum(v.astype(F32) for v in values)


def local(
    gated_hidden_input,
    frozen,
    head_gradient_rows,
    down_factor_weight,
    up_factor_weight,
    final_norm_gain,
    logratio,
    starts,
):
    row_block = frozen.shape[2]
    yh, yl, core = lax.axis_index("yh"), lax.axis_index("yl"), lax.axis_index("c")
    place = jnp.stack([lax.axis_index("z"), yh * 2 + yl, lax.axis_index("x"), core])

    positions = (yl * 2 + core) * row_block + lax.broadcasted_iota(
        jnp.int32, (1, 1, row_block), 2
    )
    partial = jnp.sum(jnp.where(positions >= starts[:, :, None], logratio, 0.0), axis=2)[0]
    high = lax.reduce_precision(partial, 8, 7)
    middle = lax.reduce_precision(partial - high, 8, 7)
    low = partial - high - middle
    sums = jnp.stack([high, middle, low], axis=1).reshape(1, 6).astype(BF)

    begin = core * 32 + yl * 16
    rows_of_down = lax.dynamic_slice_in_dim(down_factor_weight.T, begin, 16, axis=0)
    rows_of_up = lax.dynamic_slice_in_dim(up_factor_weight, begin, 16, axis=0)
    gain_part = lax.dynamic_slice_in_dim(final_norm_gain, (core * 2 + yl) * 32, 32)
    tail = jnp.concatenate([gain_part[None], sums, jnp.zeros((1, LANES - SUMS_AT - 6), BF)], axis=1)
    quarter = jnp.concatenate(
        [rows_of_up, rows_of_down, jnp.broadcast_to(tail, (16, tail.shape[1]))], axis=1
    )
    by_z = spread(quarter, "z", 8)
    near, far = together(by_z[:4], by_z[4:])
    near_parts = [ring(near, Y, 4, s) for s in (1, 2, 3)]
    far_parts = [ring(far, "x", 4, s) for s in (1, 2, 3)]
    moved = together(near, far, *near_parts, *far_parts)
    near = jnp.stack([moved[0], *moved[2:5]]).reshape(16, 16, LANES)
    far = jnp.stack([moved[1], *moved[5:8]]).reshape(16, 16, LANES)
    near, far = together(near, far)
    far_rows = [far] + [ring(far, Y, 4, s) for s in (1, 2, 3)]
    near_all = spread(near, "x", 4).reshape(64, 16, LANES)
    own = [near_all, *far_rows]
    other = [ring(v, "c", 2, 1) for v in own]

    own, other, margin = shares(
        place,
        starts,
        [*own, *other],
        gated_hidden_input.reshape(-1, gated_hidden_input.shape[3]),
        frozen.reshape(-1, frozen.shape[3]),
        head_gradient_rows.reshape(-1, frozen.shape[3]),
    )

    came = [ring(v, "c", 2, 1) for v in other]
    chip = [total_of(a, b).astype(BF) for a, b in zip(own, came)]
    far_rows = [ring(chip[1 + s], Y, 4, s) for s in (1, 2, 3)]
    near_all = lax.all_to_all(chip[0].reshape(4, 16, 16, LANES), "x", 0, 0, tiled=True)
    near = jnp.sum(near_all.astype(F32), axis=0).astype(BF).reshape(4, 4, 16, LANES)
    far = total_of(chip[1], *far_rows).astype(BF).reshape(4, 4, 16, LANES)
    near, far = together(near, far)
    near_parts = [ring(near[s], Y, 4, s) for s in (1, 2, 3)]
    far_parts = [ring(far[s], "x", 4, s) for s in (1, 2, 3)]
    moved = together(*near_parts, *far_parts)
    near = total_of(near[0], *moved[:3]).astype(BF)
    far = total_of(far[0], *moved[3:]).astype(BF)
    by_z = lax.all_to_all(jnp.concatenate([near, far]), "z", 0, 0, tiled=True)
    share = jnp.sum(by_z.astype(F32), axis=0)
    whole = spread(share, CTX, 4).reshape(2, 2, 16, LANES).transpose(1, 0, 2, 3)
    whole = whole.reshape(ORDER, LANES)
    return (
        jnp.logaddexp(0.0, -margin),
        whole[:, UP : UP + DOWN].T,
        whole[:, :UP],
    )


def solution(mesh):
    fine = Mesh(mesh.devices.reshape(FINE_SHAPE), FINE_AXES)
    return jax.shard_map(
        local,
        mesh=fine,
        in_specs=(
            P(DP, None, CTX, None),
            P(DP, None, CTX, None),
            P(DP, None, CTX, None),
            P(DP, None),
            P(None, DP),
            P(DP),
            P(DP, None, CTX),
            P(DP, None),
        ),
        out_specs=(P(DP), P(DP, None), P(None, DP)),
        check_vma=False,
    )
```

```python
import itertools

import jax
import jax.numpy as jnp
from jax import lax
from jax.experimental import pallas as pl
from jax.experimental.pallas import tpu as pltpu
from jax.sharding import Mesh, PartitionSpec as P

SCALE = 2.0
BETA = 0.1
EPS = 1e-06

FINE_AXES = ("z", "yh", "x", "yl", "c")
FINE_SHAPE = (8, 2, 4, 2, 2)
DP = ("z", "yh", "x")
CTX = ("yl", "c")

LANES = 640
UP = 128
DOWN = 462
GAIN_AT = UP + DOWN
SUMS_AT = GAIN_AT + 32
CHUNKS = 64
ORDER = 64
BF, F32 = jnp.bfloat16, jnp.float32
NT = (((1,), (1,)), ((), ()))
NN = (((1,), (0,)), ((), ()))


def dot(a, b, dims):
    return lax.dot_general(a, b, dims, preferred_element_type=F32)


def slots(place, sign):
    py, px, pc = place[1], place[2], place[3]
    dxs = [((sign * (px - x)) & 3) * 32 for x in range(4)]
    dys = [((sign * (py - y)) & 3) * 32 for y in range(4)]
    cores = [((pc + c) & 1) * 128 for c in range(2)]

    def flat(chunk, q):
        z, yh, x = chunk // 8, chunk // 4 % 2, chunk % 4
        c, y = q // 2, yh * 2 + q % 2
        if c == 0:
            return cores[0] + dxs[x] + (z * 4 + y)
        return cores[1] + dys[y] + (z * 4 + x)

    return flat


def kernel(place_ref, starts_ref, *refs):
    parts, (hidden_hbm, frozen_hbm, head_hbm) = refs[:8], refs[8:11]
    outs, margin_ref = refs[11:19], refs[19]
    hid, fro, hea, wt, up, gains, gain, pol, block, sems = refs[20:]
    width = fro.shape[1]

    loads = [
        pltpu.make_async_copy(parts[i], block.at[pl.ds(32 * i, 32)], sems.at[i]) for i in range(8)
    ]
    loads.append(pltpu.make_async_copy(hidden_hbm, hid, sems.at[8]))
    loads.append(pltpu.make_async_copy(frozen_hbm, fro, sems.at[9]))
    loads.append(pltpu.make_async_copy(head_hbm, hea, sems.at[10]))
    for copy in loads:
        copy.start()
    for copy in loads[:8]:
        copy.wait()

    pz, py, px, pc = (place_ref[i] for i in range(4))
    sums = jnp.zeros((1, 128), F32)
    for c in range(2):
        for yl in range(2):
            y = (py & 2) + yl
            inside = pz * 4 + px + ((py - y) & 3) * 32 if c else pz * 4 + y
            held = block[((pc + c) & 1) * 128 + inside]
            sums += held[0:1, LANES - 128 :].astype(F32)
    lane = SUMS_AT - (LANES - 128)
    sides = [sum(sums[:, lane + 3 * s + j : lane + 3 * s + j + 1] for j in range(3)) for s in (0, 1)]
    margin = BETA * (sides[0] - sides[1])
    margin_ref[...] = jnp.broadcast_to(margin, margin_ref.shape)
    row = lax.broadcasted_iota(jnp.int32, (128, 1), 0)
    position = (row & 63) + ((py & 1) * 2 + pc) * 64
    start = jnp.where(row < 64, starts_ref[0, 0], starts_ref[0, 1])
    weight = jnp.where(row < 64, -BETA, BETA)
    slope = jnp.where(position >= start, weight, 0.0) / (1.0 + jnp.exp(margin))

    source = slots(place_ref, 1)
    for chunk in range(CHUNKS):
        for q in range(4):
            held = block[source(chunk, q)]
            rows = slice(16 * q, 16 * q + 16)
            up[rows, chunk * UP : (chunk + 1) * UP] = held[:, :UP]
            wt[rows, chunk * DOWN : (chunk + 1) * DOWN] = held[:, UP : UP + DOWN]
            gains[q, chunk : chunk + 1, :] = held[0:1, LANES - 128 :].astype(F32)
    lane = GAIN_AT - (LANES - 128)
    gain[...] = jnp.concatenate([gains[q][:, lane : lane + 32] for q in range(4)], axis=1)

    loads[8].wait()
    tile = 2688

    def low_step(i, total):
        at = pl.ds(pl.multiple_of(i * tile, 128), tile)
        return total + dot(hid[:, at], wt[:, at], NT)

    low = lax.fori_loop(0, wt.shape[1] // tile, low_step, jnp.zeros((128, ORDER), F32)).astype(BF)
    low_t = low.astype(F32).T.astype(BF)

    loads[9].wait()
    loads[10].wait()
    step = 512

    def gained(i):
        pieces = []
        for j in range(step // 128):
            at = pl.ds(pl.multiple_of(i * step + j * 128, 128), 128)
            pieces.append(hea[:, at].astype(F32) * gain[pl.ds(i * (step // 128) + j, 1), :])
        return jnp.concatenate(pieces, axis=1)

    def fold(v):
        return sum(v[:, 128 * j : 128 * j + 128] for j in range(step // 128))

    def state_step(i, carry):
        squares, inner = carry
        at = pl.ds(pl.multiple_of(i * step, 128), step)
        state = fro[:, at].astype(F32) + SCALE * dot(low, up[:, at], NN)
        pol[:, at] = state
        return squares + fold(state * state), inner + fold(gained(i) * state)

    zero = jnp.zeros((128, 128), F32)
    squares, inner = lax.fori_loop(0, width // step, state_step, (zero, zero))
    rms = jnp.sqrt(jnp.sum(squares, axis=1, keepdims=True) / width + EPS)
    inner = slope * jnp.sum(inner, axis=1, keepdims=True)
    first = slope / rms
    second = inner / (width * rms * rms * rms)

    target = slots(place_ref, -1)
    total = jnp.zeros((128, ORDER), F32)
    for i in range(width // step):
        at = slice(i * step, (i + 1) * step)
        grad = gained(i) * first - pol[:, at] * second
        high = grad.astype(BF)
        rest = (grad - high.astype(F32)).astype(BF)
        total += dot(high, up[:, at], NT) + dot(rest, up[:, at], NT)
        share = (SCALE * dot(low_t, high, NN)).astype(BF)
        for j in range(step // 128):
            for q in range(4):
                block[target(i * (step // 128) + j, q), :, :UP] = share[
                    16 * q : 16 * q + 16, 128 * j : 128 * j + 128
                ]
    grad_low = (SCALE * total).T.astype(BF)

    for chunk in range(CHUNKS):
        begin = chunk * DOWN // 128 * 128
        shift = chunk * DOWN - begin
        span = 512 if shift + DOWN <= 512 else 640
        share = dot(grad_low, hid[:, begin : begin + span], NN)
        if shift:
            share = pltpu.roll(share, span - shift, 1)
        share = share[:, :512].astype(BF)
        for q in range(4):
            block[target(chunk, q), :, UP:] = share[16 * q : 16 * q + 16]

    stores = [
        pltpu.make_async_copy(block.at[pl.ds(32 * i, 32)], outs[i], sems.at[i]) for i in range(8)
    ]
    for copy in stores:
        copy.start()
    for copy in stores:
        copy.wait()


def shares(place, starts, parts, hidden, frozen, head):
    rows, units = hidden.shape
    width = frozen.shape[1]
    any_space = pl.BlockSpec(memory_space=pl.ANY)
    smem = pl.BlockSpec(memory_space=pltpu.SMEM)
    outs = pl.pallas_call(
        kernel,
        out_shape=[jax.ShapeDtypeStruct((32, 16, LANES), BF)] * 8
        + [jax.ShapeDtypeStruct((8, 128), F32)],
        in_specs=[smem, smem] + [any_space] * 11,
        out_specs=[any_space] * 8 + [pl.BlockSpec(memory_space=pltpu.VMEM)],
        scratch_shapes=[
            pltpu.VMEM((rows, units), BF),
            pltpu.VMEM((rows, width), BF),
            pltpu.VMEM((rows, width), BF),
            pltpu.VMEM((ORDER, units), BF),
            pltpu.VMEM((ORDER, width), BF),
            pltpu.VMEM((4, CHUNKS, 128), F32),
            pltpu.VMEM((CHUNKS, 128), F32),
            pltpu.VMEM((rows, width), F32),
            pltpu.VMEM((256, 16, LANES), BF),
            pltpu.SemaphoreType.DMA((11,)),
        ],
        compiler_params=pltpu.CompilerParams(vmem_limit_bytes=40 * 1024 * 1024),
        cost_estimate=pl.CostEstimate(
            flops=2 * rows * ORDER * (2 * units + 4 * width),
            bytes_accessed=2 * rows * (units + 2 * width) + 4 * 256 * 16 * LANES,
            transcendentals=0,
        ),
    )(place, starts, *parts, hidden, frozen, head)
    return outs[:4], outs[4:8], outs[8][0, 0:1]


def device(z, y, x, c):
    return (((z * 2 + y // 2) * 4 + x) * 2 + y % 2) * 2 + c


def ring(values, step):
    pairs = [
        (device(z, y, x, c), device(z, (y + step * c) % 4, (x + step * (1 - c)) % 4, c))
        for z, y, x, c in itertools.product(range(8), range(4), range(4), range(2))
    ]
    return lax.ppermute(values, FINE_AXES, pairs)


def crosswise(values):
    groups = [[device(z, y, x, 0) for z in range(8) for y in range(4)] for x in range(4)]
    groups += [[device(z, y, x, 1) for z in range(8) for x in range(4)] for y in range(4)]
    return lax.all_to_all(values, FINE_AXES, 0, 0, axis_index_groups=groups, tiled=True)


def other_core(values):
    return lax.ppermute(values, "c", [(0, 1), (1, 0)])


def total_of(*values):
    return sum(v.astype(F32) for v in values)


def local(
    gated_hidden_input,
    frozen,
    head_gradient_rows,
    down_factor_weight,
    up_factor_weight,
    final_norm_gain,
    logratio,
    starts,
):
    row_block = frozen.shape[2]
    yh, yl, core = lax.axis_index("yh"), lax.axis_index("yl"), lax.axis_index("c")
    place = jnp.stack([lax.axis_index("z"), yh * 2 + yl, lax.axis_index("x"), core])

    positions = (yl * 2 + core) * row_block + lax.broadcasted_iota(
        jnp.int32, (1, 1, row_block), 2
    )
    partial = jnp.sum(jnp.where(positions >= starts[:, :, None], logratio, 0.0), axis=2)[0]
    high = lax.reduce_precision(partial, 8, 7)
    middle = lax.reduce_precision(partial - high, 8, 7)
    low = partial - high - middle
    sums = jnp.stack([high, middle, low], axis=1).reshape(1, 6).astype(BF)

    begin = core * 32 + yl * 16
    rows_of_down = lax.dynamic_slice_in_dim(down_factor_weight.T, begin, 16, axis=0)
    rows_of_up = lax.dynamic_slice_in_dim(up_factor_weight, begin, 16, axis=0)
    gain_part = lax.dynamic_slice_in_dim(final_norm_gain, (core * 2 + yl) * 32, 32)
    tail = jnp.concatenate([gain_part[None], sums, jnp.zeros((1, LANES - SUMS_AT - 6), BF)], axis=1)
    quarter = jnp.concatenate(
        [rows_of_up, rows_of_down, jnp.broadcast_to(tail, (16, tail.shape[1]))], axis=1
    )
    held = crosswise(jnp.broadcast_to(quarter[None], (32, 16, LANES)))
    own = [held] + [ring(held, step) for step in (1, 2, 3)]
    other = [other_core(v) for v in own]

    own, other, margin = shares(
        place,
        starts,
        [*own, *other],
        gated_hidden_input.reshape(-1, gated_hidden_input.shape[3]),
        frozen.reshape(-1, frozen.shape[3]),
        head_gradient_rows.reshape(-1, frozen.shape[3]),
    )

    chip = [total_of(a, other_core(b)).astype(BF) for a, b in zip(own, other)]
    came = [ring(chip[step], step) for step in (1, 2, 3)]
    line = total_of(chip[0], *came).astype(BF)
    share = jnp.sum(crosswise(line).astype(F32), axis=0)
    copies = jnp.broadcast_to(share[None], (4, 16, LANES))
    whole = lax.all_to_all(copies, CTX, 0, 0, tiled=True)
    whole = whole.reshape(2, 2, 16, LANES).transpose(1, 0, 2, 3)
    whole = whole.reshape(ORDER, LANES)
    return (
        jnp.logaddexp(0.0, -margin),
        whole[:, UP : UP + DOWN].T,
        whole[:, :UP],
    )


def solution(mesh):
    fine = Mesh(mesh.devices.reshape(FINE_SHAPE), FINE_AXES)
    return jax.shard_map(
        local,
        mesh=fine,
        in_specs=(
            P(DP, None, CTX, None),
            P(DP, None, CTX, None),
            P(DP, None, CTX, None),
            P(DP, None),
            P(None, DP),
            P(DP),
            P(DP, None, CTX),
            P(DP, None),
        ),
        out_specs=(P(DP), P(DP, None), P(None, DP)),
        check_vma=False,
    )
```

```python
import itertools

import jax
import jax.numpy as jnp
from jax import lax
from jax.experimental import pallas as pl
from jax.experimental.pallas import tpu as pltpu
from jax.sharding import Mesh, PartitionSpec as P

SCALE = 2.0
BETA = 0.1
EPS = 1e-06

FINE_AXES = ("z", "yh", "x", "yl", "c")
FINE_SHAPE = (8, 2, 4, 2, 2)
DP = ("z", "yh", "x")
CTX = ("yl", "c")

LANES = 640
UP = 128
DOWN = 462
GAIN_AT = UP + DOWN
SUMS_AT = GAIN_AT + 32
CHUNKS = 64
ORDER = 64
BF, F32 = jnp.bfloat16, jnp.float32
NT = (((1,), (1,)), ((), ()))
NN = (((1,), (0,)), ((), ()))


def dot(a, b, dims):
    return lax.dot_general(a, b, dims, preferred_element_type=F32)


def slots(place, sign):
    py, px, pc = place[1], place[2], place[3]
    dxs = [((sign * (px - x)) & 3) * 32 for x in range(4)]
    dys = [((sign * (py - y)) & 3) * 32 for y in range(4)]

    def flat(chunk, other, yl):
        z, yh, x = chunk // 8, chunk // 4 % 2, chunk % 4
        y = yh * 2 + yl
        first = pc == other
        return jnp.where(first, dxs[x] + (z * 4 + y), dys[y] + (z * 4 + x))

    return flat


def kernel(place_ref, starts_ref, *refs):
    parts, (hid, fro, hea) = refs[:8], refs[8:11]
    outs, margin_ref = refs[11:13], refs[13]
    wt, up, gains, gain, pol, block, sems = refs[14:]
    width = fro.shape[1]

    loads = [
        pltpu.make_async_copy(parts[i], block.at[pl.ds(32 * i, 32)], sems.at[i]) for i in range(8)
    ]
    for copy in loads:
        copy.start()
    for copy in loads:
        copy.wait()

    pz, py, px, pc = (place_ref[i] for i in range(4))
    sums = jnp.zeros((1, 128), F32)
    for other in range(2):
        for yl in range(2):
            y = (py & 2) + yl
            inside = jnp.where(pc == other, pz * 4 + y, pz * 4 + px + ((py - y) & 3) * 32)
            held = block[other * 128 + inside]
            sums += held[0:1, LANES - 128 :].astype(F32)
    lane = SUMS_AT - (LANES - 128)
    sides = [sum(sums[:, lane + 3 * s + j : lane + 3 * s + j + 1] for j in range(3)) for s in (0, 1)]
    margin = BETA * (sides[0] - sides[1])
    margin_ref[...] = jnp.broadcast_to(margin, margin_ref.shape)
    row = lax.broadcasted_iota(jnp.int32, (128, 1), 0)
    position = (row & 63) + ((py & 1) * 2 + pc) * 64
    start = jnp.where(row < 64, starts_ref[0, 0], starts_ref[0, 1])
    weight = jnp.where(row < 64, -BETA, BETA)
    slope = jnp.where(position >= start, weight, 0.0) / (1.0 + jnp.exp(margin))

    source = slots(place_ref, 1)
    for chunk in range(CHUNKS):
        for q in range(4):
            held = block[(q // 2) * 128 + source(chunk, q // 2, q % 2)]
            rows = slice(16 * q, 16 * q + 16)
            up[rows, chunk * UP : (chunk + 1) * UP] = held[:, :UP]
            wt[rows, chunk * DOWN : (chunk + 1) * DOWN] = held[:, UP : UP + DOWN]
            gains[q, chunk : chunk + 1, :] = held[0:1, LANES - 128 :].astype(F32)
    lane = GAIN_AT - (LANES - 128)
    parts_of_gain = [gains[q][:, lane : lane + 32] for q in range(4)]
    ordered = jnp.concatenate(parts_of_gain, axis=1)
    swapped = jnp.concatenate(parts_of_gain[2:] + parts_of_gain[:2], axis=1)
    gain[...] = jnp.where(pc == 0, ordered, swapped)

    tile = 5888
    main = wt.shape[1] // tile
    low = dot(hid[:, main * tile :], wt[:, main * tile :], NT)
    for i in range(main):
        at = slice(i * tile, i * tile + tile)
        low += dot(hid[:, at], wt[:, at], NT)
    low = low.astype(BF)
    low_t = low.astype(F32).T.astype(BF)

    step = 512

    def gained(i):
        pieces = []
        for j in range(step // 128):
            at = slice(i * step + j * 128, i * step + j * 128 + 128)
            chunk = i * (step // 128) + j
            pieces.append(hea[:, at].astype(F32) * gain[chunk : chunk + 1, :])
        return jnp.concatenate(pieces, axis=1)

    def fold(v):
        return sum(v[:, 128 * j : 128 * j + 128] for j in range(step // 128))

    def state_step(i, carry):
        squares, inner = carry
        at = slice(i * step, i * step + step)
        state = fro[:, at].astype(F32) + SCALE * dot(low, up[:, at], NN)
        pol[:, at] = state
        return squares + fold(state * state), inner + fold(gained(i) * state)

    zero = jnp.zeros((128, 128), F32)
    squares, inner = zero, zero
    for i in range(width // step):
        squares, inner = state_step(i, (squares, inner))
    rms = jnp.sqrt(jnp.sum(squares, axis=1, keepdims=True) / width + EPS)
    inner = slope * jnp.sum(inner, axis=1, keepdims=True)
    first = slope / rms
    second = inner / (width * rms * rms * rms)

    target = slots(place_ref, -1)
    total = jnp.zeros((128, ORDER), F32)
    for i in range(width // step):
        at = slice(i * step, (i + 1) * step)
        grad = gained(i) * first - pol[:, at] * second
        high = grad.astype(BF)
        rest = (grad - high.astype(F32)).astype(BF)
        total += dot(high, up[:, at], NT) + dot(rest, up[:, at], NT)
        share = (SCALE * dot(low_t, high, NN)).astype(BF)
        for j in range(step // 128):
            for q in range(4):
                outs[q // 2][target(i * (step // 128) + j, q // 2, q % 2), :, :UP] = share[
                    16 * q : 16 * q + 16, 128 * j : 128 * j + 128
                ]
    grad_low = (SCALE * total).T.astype(BF)

    tile = 1024
    for begin in range(0, wt.shape[1], tile):
        at = slice(begin, min(begin + tile, wt.shape[1]))
        wt[:, at] = dot(grad_low, hid[:, at], NN).astype(BF)
    for chunk in range(CHUNKS):
        for q in range(4):
            outs[q // 2][target(chunk, q // 2, q % 2), :, UP : UP + DOWN] = wt[
                16 * q : 16 * q + 16, chunk * DOWN : (chunk + 1) * DOWN
            ]


def bring(after_ref, *refs):
    sems = refs[6]
    copies = [pltpu.make_async_copy(refs[i], refs[3 + i], sems.at[i]) for i in range(3)]
    for copy in copies:
        copy.start()
    for copy in copies:
        copy.wait()


def brought(after, *arrays):
    any_space = pl.BlockSpec(memory_space=pl.ANY)
    size = sum(v.size * 2 for v in arrays)
    return pl.pallas_call(
        bring,
        out_shape=[pltpu.VMEM(v.shape, v.dtype) for v in arrays],
        in_specs=[any_space] * 4,
        out_specs=[pl.BlockSpec(memory_space=pltpu.VMEM)] * 3,
        scratch_shapes=[pltpu.SemaphoreType.DMA((3,))],
        compiler_params=pltpu.CompilerParams(vmem_limit_bytes=1024 * 1024),
        cost_estimate=pl.CostEstimate(flops=0, bytes_accessed=2 * size, transcendentals=0),
    )(after, *[pltpu.with_memory_space_constraint(v, pltpu.HBM) for v in arrays])


def shares(place, starts, parts, hidden, frozen, head):
    rows, units = hidden.shape
    width = frozen.shape[1]
    any_space = pl.BlockSpec(memory_space=pl.ANY)
    smem = pl.BlockSpec(memory_space=pltpu.SMEM)
    vmem = pl.BlockSpec(memory_space=pltpu.VMEM)
    near = [pltpu.with_memory_space_constraint(v, pltpu.VMEM) for v in (hidden, frozen, head)]
    outs = pl.pallas_call(
        kernel,
        out_shape=[pltpu.VMEM((128, 16, LANES), BF)] * 2 + [jax.ShapeDtypeStruct((8, 128), F32)],
        in_specs=[smem, smem] + [any_space] * 8 + [vmem] * 3,
        out_specs=[vmem] * 3,
        scratch_shapes=[
            pltpu.VMEM((ORDER, units), BF),
            pltpu.VMEM((ORDER, width), BF),
            pltpu.VMEM((4, CHUNKS, 128), F32),
            pltpu.VMEM((CHUNKS, 128), F32),
            pltpu.VMEM((rows, width), F32),
            pltpu.VMEM((256, 16, LANES), BF),
            pltpu.SemaphoreType.DMA((8,)),
        ],
        compiler_params=pltpu.CompilerParams(vmem_limit_bytes=24 * 1024 * 1024),
        cost_estimate=pl.CostEstimate(
            flops=2 * rows * ORDER * (2 * units + 4 * width),
            bytes_accessed=2 * rows * (units + 2 * width) + 4 * 256 * 16 * LANES,
            transcendentals=0,
        ),
    )(place, starts, *parts, *near)
    return outs[0], outs[1], outs[2][0, 0:1]


def device(z, y, x, c):
    return (((z * 2 + y // 2) * 4 + x) * 2 + y % 2) * 2 + c


def ring(values, step):
    pairs = [
        (device(z, y, x, c), device(z, (y + step * c) % 4, (x + step * (1 - c)) % 4, c))
        for z, y, x, c in itertools.product(range(8), range(4), range(4), range(2))
    ]
    return lax.ppermute(values, FINE_AXES, pairs)


def crosswise(values):
    groups = [[device(z, y, x, 0) for z in range(8) for y in range(4)] for x in range(4)]
    groups += [[device(z, y, x, 1) for z in range(8) for x in range(4)] for y in range(4)]
    return lax.all_to_all(values, FINE_AXES, 0, 0, axis_index_groups=groups, tiled=True)


def other_core(values):
    return lax.ppermute(values, "c", [(0, 1), (1, 0)])


def total_of(*values):
    return sum(v.astype(F32) for v in values)


def local(
    gated_hidden_input,
    frozen,
    head_gradient_rows,
    down_factor_weight,
    up_factor_weight,
    final_norm_gain,
    logratio,
    starts,
):
    row_block = frozen.shape[2]
    yh, yl, core = lax.axis_index("yh"), lax.axis_index("yl"), lax.axis_index("c")
    place = jnp.stack([lax.axis_index("z"), yh * 2 + yl, lax.axis_index("x"), core])

    positions = (yl * 2 + core) * row_block + lax.broadcasted_iota(
        jnp.int32, (1, 1, row_block), 2
    )
    partial = jnp.sum(jnp.where(positions >= starts[:, :, None], logratio, 0.0), axis=2)[0]
    high = lax.reduce_precision(partial, 8, 7)
    middle = lax.reduce_precision(partial - high, 8, 7)
    low = partial - high - middle
    sums = jnp.stack([high, middle, low], axis=1).reshape(1, 6).astype(BF)

    begin = core * 32 + yl * 16
    rows_of_down = lax.dynamic_slice_in_dim(down_factor_weight.T, begin, 16, axis=0)
    rows_of_up = lax.dynamic_slice_in_dim(up_factor_weight, begin, 16, axis=0)
    gain_part = lax.dynamic_slice_in_dim(final_norm_gain, (core * 2 + yl) * 32, 32)
    tail = jnp.concatenate([gain_part[None], sums, jnp.zeros((1, LANES - SUMS_AT - 6), BF)], axis=1)
    quarter = jnp.concatenate(
        [rows_of_up, rows_of_down, jnp.broadcast_to(tail, (16, tail.shape[1]))], axis=1
    )
    held = crosswise(jnp.broadcast_to(quarter[None], (32, 16, LANES)))
    own = [held] + [ring(held, step) for step in (1, 2, 3)]
    width = frozen.shape[3]
    near = brought(
        held,
        gated_hidden_input.reshape(-1, gated_hidden_input.shape[3]),
        frozen.reshape(-1, width),
        head_gradient_rows.reshape(-1, width),
    )
    held, *near = lax.optimization_barrier((held, *near))
    other = [other_core(v) for v in (held, *own[1:])]

    own, other, margin = shares(place, starts, [*own, *other], *near)

    came = other_core(other)
    chip = [
        total_of(own[32 * i : 32 * i + 32], came[32 * i : 32 * i + 32]).astype(BF)
        for i in range(4)
    ]
    came = [ring(chip[step], step) for step in (1, 2, 3)]
    line = total_of(chip[0], *came).astype(BF)
    share = jnp.sum(crosswise(line).astype(F32), axis=0)
    copies = jnp.broadcast_to(share[None], (4, 16, LANES))
    whole = lax.all_to_all(copies, CTX, 0, 0, tiled=True)
    whole = whole.reshape(2, 2, 16, LANES).transpose(1, 0, 2, 3)
    whole = whole.reshape(ORDER, LANES)
    return (
        jnp.logaddexp(0.0, -margin),
        whole[:, UP : UP + DOWN].T,
        whole[:, :UP],
    )


def solution(mesh):
    fine = Mesh(mesh.devices.reshape(FINE_SHAPE), FINE_AXES)
    return jax.shard_map(
        local,
        mesh=fine,
        in_specs=(
            P(DP, None, CTX, None),
            P(DP, None, CTX, None),
            P(DP, None, CTX, None),
            P(DP, None),
            P(None, DP),
            P(DP),
            P(DP, None, CTX),
            P(DP, None),
        ),
        out_specs=(P(DP), P(DP, None), P(None, DP)),
        check_vma=False,
    )
```

```python
import itertools

import jax
import jax.numpy as jnp
from jax import lax
from jax.experimental import pallas as pl
from jax.experimental.pallas import tpu as pltpu
from jax.sharding import Mesh, PartitionSpec as P

SCALE = 2.0
BETA = 0.1
EPS = 1e-06

FINE_AXES = ("z", "yh", "x", "yl", "c")
FINE_SHAPE = (8, 2, 4, 2, 2)
DP = ("z", "yh", "x")
CTX = ("yl", "c")

LANES = 640
UP = 128
DOWN = 462
GAIN_AT = UP + DOWN
SUMS_AT = GAIN_AT + 32
CHUNKS = 64
ORDER = 64
BF, F32 = jnp.bfloat16, jnp.float32
NT = (((1,), (1,)), ((), ()))
NN = (((1,), (0,)), ((), ()))


def dot(a, b, dims):
    return lax.dot_general(a, b, dims, preferred_element_type=F32)


def slots(place, sign, planes):
    py, px, pc = place[1], place[2], place[3]
    dxs = [((sign * (px - x)) & 3) * (planes * 4) for x in range(4)]
    dys = [((sign * (py - y)) & 3) * (planes * 4) for y in range(4)]

    def flat(chunk, other, yl):
        z, yh, x = chunk // 8 % planes, chunk // 4 % 2, chunk % 4
        y = yh * 2 + yl
        first = pc == other
        return jnp.where(first, dxs[x] + (z * 4 + y), dys[y] + (z * 4 + x))

    return flat


def down_gradient(chunks, grad_low, hid, held, outs, target):
    origin = chunks[0] * DOWN // 128 * 128
    stop = -(-(chunks[-1] + 1) * DOWN // 128) * 128
    for begin in range(origin, stop, 1024):
        end = min(begin + 1024, stop)
        held[:, begin - origin : end - origin] = dot(grad_low, hid[:, begin:end], NN).astype(BF)
    for chunk in chunks:
        begin = chunk * DOWN - origin
        for q in range(4):
            outs[q // 2][target(chunk, q // 2, q % 2), :, UP : UP + DOWN] = held[
                16 * q : 16 * q + 16, begin : begin + DOWN
            ]


def kernel(place_ref, starts_ref, *refs):
    parts, (hid, fro, hea) = refs[:8], refs[8:11]
    outs, up_rest, low_ref, margin_ref = refs[11:13], refs[13], refs[14], refs[15]
    wt, up, gains, gain, pol, block, sems = refs[16:]
    width = fro.shape[1]

    loads = [
        pltpu.make_async_copy(parts[i], block.at[pl.ds(32 * i, 32)], sems.at[i]) for i in range(8)
    ]
    for copy in loads:
        copy.start()
    for copy in loads:
        copy.wait()

    pz, py, px, pc = (place_ref[i] for i in range(4))
    sums = jnp.zeros((1, 128), F32)
    for other in range(2):
        for yl in range(2):
            y = (py & 2) + yl
            inside = jnp.where(pc == other, pz * 4 + y, pz * 4 + px + ((py - y) & 3) * 32)
            held = block[other * 128 + inside]
            sums += held[0:1, LANES - 128 :].astype(F32)
    lane = SUMS_AT - (LANES - 128)
    sides = [sum(sums[:, lane + 3 * s + j : lane + 3 * s + j + 1] for j in range(3)) for s in (0, 1)]
    margin = BETA * (sides[0] - sides[1])
    margin_ref[...] = jnp.broadcast_to(margin, margin_ref.shape)
    row = lax.broadcasted_iota(jnp.int32, (128, 1), 0)
    position = (row & 63) + ((py & 1) * 2 + pc) * 64
    start = jnp.where(row < 64, starts_ref[0, 0], starts_ref[0, 1])
    weight = jnp.where(row < 64, -BETA, BETA)
    slope = jnp.where(position >= start, weight, 0.0) / (1.0 + jnp.exp(margin))

    source = slots(place_ref, 1, 8)
    for chunk in range(CHUNKS):
        for q in range(4):
            held = block[(q // 2) * 128 + source(chunk, q // 2, q % 2)]
            rows = slice(16 * q, 16 * q + 16)
            up[rows, chunk * UP : (chunk + 1) * UP] = held[:, :UP]
            wt[rows, chunk * DOWN : (chunk + 1) * DOWN] = held[:, UP : UP + DOWN]
            gains[q, chunk : chunk + 1, :] = held[0:1, LANES - 128 :].astype(F32)
    lane = GAIN_AT - (LANES - 128)
    parts_of_gain = [gains[q][:, lane : lane + 32] for q in range(4)]
    ordered = jnp.concatenate(parts_of_gain, axis=1)
    swapped = jnp.concatenate(parts_of_gain[2:] + parts_of_gain[:2], axis=1)
    gain[...] = jnp.where(pc == 0, ordered, swapped)

    tile = 5888
    main = wt.shape[1] // tile
    low = dot(hid[:, main * tile :], wt[:, main * tile :], NT)
    for i in range(main):
        at = slice(i * tile, i * tile + tile)
        low += dot(hid[:, at], wt[:, at], NT)
    low = low.astype(BF)
    low_t = low.astype(F32).T.astype(BF)

    step = 512

    def gained(i):
        pieces = []
        for j in range(step // 128):
            at = slice(i * step + j * 128, i * step + j * 128 + 128)
            chunk = i * (step // 128) + j
            pieces.append(hea[:, at].astype(F32) * gain[chunk : chunk + 1, :])
        return jnp.concatenate(pieces, axis=1)

    def fold(v):
        return sum(v[:, 128 * j : 128 * j + 128] for j in range(step // 128))

    def state_step(i, carry):
        squares, inner = carry
        at = slice(i * step, i * step + step)
        state = fro[:, at].astype(F32) + SCALE * dot(low, up[:, at], NN)
        pol[:, at] = state
        return squares + fold(state * state), inner + fold(gained(i) * state)

    zero = jnp.zeros((128, 128), F32)
    squares, inner = zero, zero
    for i in range(width // step):
        squares, inner = state_step(i, (squares, inner))
    rms = jnp.sqrt(jnp.sum(squares, axis=1, keepdims=True) / width + EPS)
    inner = slope * jnp.sum(inner, axis=1, keepdims=True)
    first = slope / rms
    second = inner / (width * rms * rms * rms)

    target = slots(place_ref, -1, 4)
    total = jnp.zeros((128, ORDER), F32)
    for i in range(width // step):
        at = slice(i * step, (i + 1) * step)
        grad = gained(i) * first - pol[:, at] * second
        high = grad.astype(BF)
        rest = (grad - high.astype(F32)).astype(BF)
        total += dot(high, up[:, at], NT) + dot(rest, up[:, at], NT)
        share = (SCALE * dot(low_t, high, NN)).astype(BF)
        if i * step >= width // 2:
            up_rest[:, i * step - width // 2 : (i + 1) * step - width // 2] = share
            continue
        for j in range(step // 128):
            for q in range(4):
                outs[q // 2][target(i * (step // 128) + j, q // 2, q % 2), :, :UP] = share[
                    16 * q : 16 * q + 16, 128 * j : 128 * j + 128
                ]
    grad_low = (SCALE * total).T.astype(BF)

    low_ref[...] = grad_low
    down_gradient(range(CHUNKS // 2), grad_low, hid, wt, outs, target)


def second_kernel(place_ref, low_ref, up_rest, hid, *refs):
    outs, held = refs[:2], refs[2]
    target = slots(place_ref, -1, 4)
    chunks = range(CHUNKS // 2, CHUNKS)
    for i, chunk in enumerate(chunks):
        for q in range(4):
            outs[q // 2][target(chunk, q // 2, q % 2), :, :UP] = up_rest[
                16 * q : 16 * q + 16, UP * i : UP * i + UP
            ]
    down_gradient(chunks, low_ref[...], hid, held, outs, target)


def bring(after_ref, place_ref, *refs):
    sems = refs[6]
    copies = [pltpu.make_async_copy(refs[i], refs[3 + i], sems.at[i]) for i in range(3)]
    for copy in copies:
        copy.start()
    for copy in copies:
        copy.wait()


def brought(after, place, *arrays):
    any_space = pl.BlockSpec(memory_space=pl.ANY)
    size = sum(v.size * 2 for v in arrays)
    return pl.pallas_call(
        bring,
        out_shape=[pltpu.VMEM(v.shape, v.dtype) for v in arrays],
        in_specs=[any_space, pl.BlockSpec(memory_space=pltpu.SMEM)] + [any_space] * 3,
        out_specs=[pl.BlockSpec(memory_space=pltpu.VMEM)] * 3,
        scratch_shapes=[pltpu.SemaphoreType.DMA((3,))],
        compiler_params=pltpu.CompilerParams(vmem_limit_bytes=1024 * 1024),
        cost_estimate=pl.CostEstimate(flops=0, bytes_accessed=2 * size, transcendentals=0),
    )(after, place, *[pltpu.with_memory_space_constraint(v, pltpu.HBM) for v in arrays])


def near_vmem(*arrays):
    return [pltpu.with_memory_space_constraint(v, pltpu.VMEM) for v in arrays]


def shares(place, starts, parts, hidden, frozen, head):
    rows, units = hidden.shape
    width = frozen.shape[1]
    any_space = pl.BlockSpec(memory_space=pl.ANY)
    smem = pl.BlockSpec(memory_space=pltpu.SMEM)
    vmem = pl.BlockSpec(memory_space=pltpu.VMEM)
    *outs, up_rest, grad_low, margin = pl.pallas_call(
        kernel,
        out_shape=[pltpu.VMEM((64, 16, LANES), BF)] * 2
        + [
            pltpu.VMEM((ORDER, width // 2), BF),
            pltpu.VMEM((ORDER, rows), BF),
            jax.ShapeDtypeStruct((8, 128), F32),
        ],
        in_specs=[smem, smem] + [any_space] * 8 + [vmem] * 3,
        out_specs=[vmem] * 5,
        scratch_shapes=[
            pltpu.VMEM((ORDER, units), BF),
            pltpu.VMEM((ORDER, width), BF),
            pltpu.VMEM((4, CHUNKS, 128), F32),
            pltpu.VMEM((CHUNKS, 128), F32),
            pltpu.VMEM((rows, width), F32),
            pltpu.VMEM((256, 16, LANES), BF),
            pltpu.SemaphoreType.DMA((8,)),
        ],
        compiler_params=pltpu.CompilerParams(vmem_limit_bytes=20 * 1024 * 1024),
        cost_estimate=pl.CostEstimate(
            flops=2 * rows * ORDER * (2 * units + 4 * width),
            bytes_accessed=2 * rows * (units + 2 * width) + 4 * 256 * 16 * LANES,
            transcendentals=0,
        ),
    )(place, starts, *parts, *near_vmem(hidden, frozen, head))
    rest = pl.pallas_call(
        second_kernel,
        out_shape=[pltpu.VMEM((64, 16, LANES), BF)] * 2,
        in_specs=[smem] + [vmem] * 3,
        out_specs=[vmem] * 2,
        scratch_shapes=[pltpu.VMEM((ORDER, (units // 256 + 1) * 128), BF)],
        compiler_params=pltpu.CompilerParams(vmem_limit_bytes=4 * 1024 * 1024),
        cost_estimate=pl.CostEstimate(
            flops=rows * ORDER * units,
            bytes_accessed=rows * units + 2 * 128 * 16 * LANES,
            transcendentals=0,
        ),
    )(place, *near_vmem(grad_low, up_rest, hidden))
    return outs, rest, margin[0, 0:1]


def device(z, y, x, c):
    return (((z * 2 + y // 2) * 4 + x) * 2 + y % 2) * 2 + c


def ring(values, step):
    pairs = [
        (device(z, y, x, c), device(z, (y + step * c) % 4, (x + step * (1 - c)) % 4, c))
        for z, y, x, c in itertools.product(range(8), range(4), range(4), range(2))
    ]
    return lax.ppermute(values, FINE_AXES, pairs)


def crosswise(values):
    groups = [[device(z, y, x, 0) for z in range(8) for y in range(4)] for x in range(4)]
    groups += [[device(z, y, x, 1) for z in range(8) for x in range(4)] for y in range(4)]
    return lax.all_to_all(values, FINE_AXES, 0, 0, axis_index_groups=groups, tiled=True)


def other_core(values):
    return lax.ppermute(values, "c", [(0, 1), (1, 0)])


def total_of(*values):
    return sum(v.astype(F32) for v in values)


def local(
    gated_hidden_input,
    frozen,
    head_gradient_rows,
    down_factor_weight,
    up_factor_weight,
    final_norm_gain,
    logratio,
    starts,
):
    row_block = frozen.shape[2]
    yh, yl, core = lax.axis_index("yh"), lax.axis_index("yl"), lax.axis_index("c")
    place = jnp.stack([lax.axis_index("z"), yh * 2 + yl, lax.axis_index("x"), core])

    positions = (yl * 2 + core) * row_block + lax.broadcasted_iota(
        jnp.int32, (1, 1, row_block), 2
    )
    partial = jnp.sum(jnp.where(positions >= starts[:, :, None], logratio, 0.0), axis=2)[0]
    high = lax.reduce_precision(partial, 8, 7)
    middle = lax.reduce_precision(partial - high, 8, 7)
    low = partial - high - middle
    sums = jnp.stack([high, middle, low], axis=1).reshape(1, 6).astype(BF)

    begin = core * 32 + yl * 16
    rows_of_down = lax.dynamic_slice_in_dim(down_factor_weight.T, begin, 16, axis=0)
    rows_of_up = lax.dynamic_slice_in_dim(up_factor_weight, begin, 16, axis=0)
    gain_part = lax.dynamic_slice_in_dim(final_norm_gain, (core * 2 + yl) * 32, 32)
    tail = jnp.concatenate([gain_part[None], sums, jnp.zeros((1, LANES - SUMS_AT - 6), BF)], axis=1)
    quarter = jnp.concatenate(
        [rows_of_up, rows_of_down, jnp.broadcast_to(tail, (16, tail.shape[1]))], axis=1
    )
    held = crosswise(jnp.broadcast_to(quarter[None], (32, 16, LANES)))
    own = [held] + [ring(held, step) for step in (1, 2, 3)]
    width = frozen.shape[3]
    near = brought(
        held,
        place,
        gated_hidden_input.reshape(-1, gated_hidden_input.shape[3]),
        frozen.reshape(-1, width),
        head_gradient_rows.reshape(-1, width),
    )
    held, *near = lax.optimization_barrier((held, *near))
    other = [other_core(v) for v in (held, *own[1:])]

    first, second, margin = shares(place, starts, [*own, *other], *near)

    lines = []
    for own, other in (first, second):
        came = other_core(other)
        chip = [
            total_of(own[16 * i : 16 * i + 16], came[16 * i : 16 * i + 16]).astype(BF)
            for i in range(4)
        ]
        came = [ring(chip[step], step) for step in (1, 2, 3)]
        lines.append(total_of(chip[0], *came).astype(BF))
    line = jnp.concatenate(lines)
    share = jnp.sum(crosswise(line).astype(F32), axis=0)
    copies = jnp.broadcast_to(share[None], (4, 16, LANES))
    whole = lax.all_to_all(copies, CTX, 0, 0, tiled=True)
    whole = whole.reshape(2, 2, 16, LANES).transpose(1, 0, 2, 3)
    whole = whole.reshape(ORDER, LANES)
    return (
        jnp.logaddexp(0.0, -margin),
        whole[:, UP : UP + DOWN].T,
        whole[:, :UP],
    )


def solution(mesh):
    fine = Mesh(mesh.devices.reshape(FINE_SHAPE), FINE_AXES)
    return jax.shard_map(
        local,
        mesh=fine,
        in_specs=(
            P(DP, None, CTX, None),
            P(DP, None, CTX, None),
            P(DP, None, CTX, None),
            P(DP, None),
            P(None, DP),
            P(DP),
            P(DP, None, CTX),
            P(DP, None),
        ),
        out_specs=(P(DP), P(DP, None), P(None, DP)),
        check_vma=False,
    )
```

```python
import itertools

import jax
import jax.numpy as jnp
from jax import lax
from jax.experimental import pallas as pl
from jax.experimental.pallas import tpu as pltpu
from jax.sharding import Mesh, PartitionSpec as P

SCALE = 2.0
BETA = 0.1
EPS = 1e-06

FINE_AXES = ("z", "yh", "x", "yl", "c")
FINE_SHAPE = (8, 2, 4, 2, 2)
DP = ("z", "yh", "x")
CTX = ("yl", "c")

LANES = 640
UP = 128
DOWN = 462
GAIN_AT = UP + DOWN
SUMS_AT = GAIN_AT + 32
CHUNKS = 64
ORDER = 64
BF, F32 = jnp.bfloat16, jnp.float32
NT = (((1,), (1,)), ((), ()))
NN = (((1,), (0,)), ((), ()))


def dot(a, b, dims):
    return lax.dot_general(a, b, dims, preferred_element_type=F32)


def slots(place, sign, planes):
    py, px, pc = place[1], place[2], place[3]
    dxs = [((sign * (px - x)) & 3) * planes for x in range(4)]
    dys = [((sign * (py - y)) & 3) * planes for y in range(4)]

    def flat(chunk, other, yl):
        z, yh, x = chunk // 8 % planes, chunk // 4 % 2, chunk % 4
        dx, dy = dxs[x], dys[yh * 2 + yl]
        return jnp.where(pc == other, dx * 4 + dy, dy * 4 + dx) + z

    return flat


def down_gradient(chunks, grad_low, hid, held, outs, target):
    origin = chunks[0] * DOWN // 128 * 128
    stop = -(-(chunks[-1] + 1) * DOWN // 128) * 128
    for begin in range(origin, stop, 1024):
        end = min(begin + 1024, stop)
        held[:, begin - origin : end - origin] = dot(grad_low, hid[:, begin:end], NN).astype(BF)
    for chunk in chunks:
        begin = chunk * DOWN - origin
        for q in range(4):
            outs[q // 2][target(chunk, q // 2, q % 2), :, UP : UP + DOWN] = held[
                16 * q : 16 * q + 16, begin : begin + DOWN
            ]


def kernel(place_ref, starts_ref, *refs):
    parts, (hid, fro, hea) = refs[:16], refs[16:19]
    outs, up_rest, low_ref, margin_ref = refs[19:21], refs[21], refs[22], refs[23]
    wt, up, gains, gain, pol, block, sems = refs[24:]
    width = fro.shape[1]

    loads = [
        pltpu.make_async_copy(
            parts[i],
            block.at[pl.ds(32 * (i // 2) + 8 * (i % 2), 8 + 16 * (i % 2))],
            sems.at[i],
        )
        for i in range(16)
    ]
    for copy in loads:
        copy.start()
    for copy in loads:
        copy.wait()

    pz, py, px, pc = (place_ref[i] for i in range(4))
    sums = jnp.zeros((1, 128), F32)
    for other in range(2):
        for yl in range(2):
            y = (py & 2) + yl
            dy = (py - y) & 3
            inside = jnp.where(pc == other, dy * 8, dy * 32) + pz
            held = block[other * 128 + inside]
            sums += held[0:1, LANES - 128 :].astype(F32)
    lane = SUMS_AT - (LANES - 128)
    sides = [sum(sums[:, lane + 3 * s + j : lane + 3 * s + j + 1] for j in range(3)) for s in (0, 1)]
    margin = BETA * (sides[0] - sides[1])
    margin_ref[...] = jnp.broadcast_to(margin, margin_ref.shape)
    row = lax.broadcasted_iota(jnp.int32, (128, 1), 0)
    position = (row & 63) + ((py & 1) * 2 + pc) * 64
    start = jnp.where(row < 64, starts_ref[0, 0], starts_ref[0, 1])
    weight = jnp.where(row < 64, -BETA, BETA)
    slope = jnp.where(position >= start, weight, 0.0) / (1.0 + jnp.exp(margin))

    source = slots(place_ref, 1, 8)
    for chunk in range(CHUNKS):
        for q in range(4):
            held = block[(q // 2) * 128 + source(chunk, q // 2, q % 2)]
            rows = slice(16 * q, 16 * q + 16)
            up[rows, chunk * UP : (chunk + 1) * UP] = held[:, :UP]
            wt[rows, chunk * DOWN : (chunk + 1) * DOWN] = held[:, UP : UP + DOWN]
            gains[q, chunk : chunk + 1, :] = held[0:1, LANES - 128 :].astype(F32)
    lane = GAIN_AT - (LANES - 128)
    parts_of_gain = [gains[q][:, lane : lane + 32] for q in range(4)]
    ordered = jnp.concatenate(parts_of_gain, axis=1)
    swapped = jnp.concatenate(parts_of_gain[2:] + parts_of_gain[:2], axis=1)
    gain[...] = jnp.where(pc == 0, ordered, swapped)

    tile = 5888
    main = wt.shape[1] // tile
    low = dot(hid[:, main * tile :], wt[:, main * tile :], NT)
    for i in range(main):
        at = slice(i * tile, i * tile + tile)
        low += dot(hid[:, at], wt[:, at], NT)
    low = low.astype(BF)
    low_t = low.astype(F32).T.astype(BF)

    step = 512

    def gained(i):
        pieces = []
        for j in range(step // 128):
            at = slice(i * step + j * 128, i * step + j * 128 + 128)
            chunk = i * (step // 128) + j
            pieces.append(hea[:, at].astype(F32) * gain[chunk : chunk + 1, :])
        return jnp.concatenate(pieces, axis=1)

    def fold(v):
        return sum(v[:, 128 * j : 128 * j + 128] for j in range(step // 128))

    def state_step(i, carry):
        squares, inner = carry
        at = slice(i * step, i * step + step)
        state = fro[:, at].astype(F32) + SCALE * dot(low, up[:, at], NN)
        pol[:, at] = state
        return squares + fold(state * state), inner + fold(gained(i) * state)

    zero = jnp.zeros((128, 128), F32)
    squares, inner = zero, zero
    for i in range(width // step):
        squares, inner = state_step(i, (squares, inner))
    rms = jnp.sqrt(jnp.sum(squares, axis=1, keepdims=True) / width + EPS)
    inner = slope * jnp.sum(inner, axis=1, keepdims=True)
    first = slope / rms
    second = inner / (width * rms * rms * rms)

    target = slots(place_ref, -1, 4)
    total = jnp.zeros((128, ORDER), F32)
    for i in range(width // step):
        at = slice(i * step, (i + 1) * step)
        grad = gained(i) * first - pol[:, at] * second
        high = grad.astype(BF)
        rest = (grad - high.astype(F32)).astype(BF)
        total += dot(high, up[:, at], NT) + dot(rest, up[:, at], NT)
        share = (SCALE * dot(low_t, high, NN)).astype(BF)
        if i * step >= width // 2:
            up_rest[:, i * step - width // 2 : (i + 1) * step - width // 2] = share
            continue
        for j in range(step // 128):
            for q in range(4):
                outs[q // 2][target(i * (step // 128) + j, q // 2, q % 2), :, :UP] = share[
                    16 * q : 16 * q + 16, 128 * j : 128 * j + 128
                ]
    grad_low = (SCALE * total).T.astype(BF)

    low_ref[...] = grad_low
    down_gradient(range(CHUNKS // 2), grad_low, hid, wt, outs, target)


def second_kernel(place_ref, low_ref, up_rest, hid, *refs):
    outs, held = refs[:2], refs[2]
    target = slots(place_ref, -1, 4)
    chunks = range(CHUNKS // 2, CHUNKS)
    for i, chunk in enumerate(chunks):
        for q in range(4):
            outs[q // 2][target(chunk, q // 2, q % 2), :, :UP] = up_rest[
                16 * q : 16 * q + 16, UP * i : UP * i + UP
            ]
    down_gradient(chunks, low_ref[...], hid, held, outs, target)


def pack(place_ref, starts_ref, ratio_ref, down_ref, up_ref, gain_ref, out_ref):
    yl, core = place_ref[1] & 1, place_ref[3]
    begin = pl.multiple_of(core * 32 + yl * 16, 16)
    position = lax.broadcasted_iota(jnp.int32, (2, 64), 1) + (yl * 2 + core) * 64
    side = lax.broadcasted_iota(jnp.int32, (2, 64), 0)
    start = jnp.where(side == 0, starts_ref[0, 0], starts_ref[0, 1])
    total = jnp.sum(jnp.where(position >= start, ratio_ref[...], 0.0), axis=1, keepdims=True)
    high = total.astype(BF).astype(F32)
    middle = (total - high).astype(BF).astype(F32)
    low = total - high - middle

    lane = lax.broadcasted_iota(jnp.int32, (8, 128), 1)
    at = GAIN_AT - (LANES - 128)
    gain = jnp.broadcast_to(gain_ref[...].astype(F32), (8, 128))
    gain = pltpu.roll(gain, (at + 128 - (core * 2 + yl) * 32) & 127, 1)
    tail = jnp.where((lane >= at) & (lane < at + 32), gain, 0.0)
    for s in range(2):
        for j, part in enumerate((high, middle, low)):
            tail = jnp.where(lane == at + 32 + 3 * s + j, part[s : s + 1], tail)
    tail = jnp.concatenate([tail, tail], axis=0).astype(BF)
    rows = pl.ds(begin, 16)
    for i in range(8):
        out_ref[i, :, :UP] = up_ref[rows, :]
        out_ref[i, :, LANES - 128 :] = tail
        out_ref[i, :, UP:GAIN_AT] = down_ref[rows, :]


def packed(place, starts, ratio, down, up, gain):
    smem = pl.BlockSpec(memory_space=pltpu.SMEM)
    vmem = pl.BlockSpec(memory_space=pltpu.VMEM)
    return pl.pallas_call(
        pack,
        out_shape=jax.ShapeDtypeStruct((8, 16, LANES), BF),
        in_specs=[smem, smem] + [vmem] * 4,
        out_specs=vmem,
        compiler_params=pltpu.CompilerParams(vmem_limit_bytes=4 * 1024 * 1024),
    )(place, starts, ratio, down, up, gain)


def finish(place_ref, *refs):
    down_ref, up_ref = refs[4:]
    for i in range(4):
        core, yl = (place_ref[3] + i // 2) & 1, (place_ref[1] + i % 2) & 1
        rows = pl.ds(pl.multiple_of(core * 32 + yl * 16, 16), 16)
        up_ref[rows, :] = refs[i][:, :UP]
        down_ref[rows, :] = refs[i][:, UP:GAIN_AT]


def finished(place, *shares_):
    vmem = pl.BlockSpec(memory_space=pltpu.VMEM)
    return pl.pallas_call(
        finish,
        out_shape=[
            jax.ShapeDtypeStruct((ORDER, DOWN), F32),
            jax.ShapeDtypeStruct((ORDER, UP), F32),
        ],
        in_specs=[pl.BlockSpec(memory_space=pltpu.SMEM)] + [vmem] * 4,
        out_specs=[vmem] * 2,
        compiler_params=pltpu.CompilerParams(vmem_limit_bytes=4 * 1024 * 1024),
    )(place, *shares_)


def bring(after_ref, place_ref, *refs):
    sems = refs[6]
    copies = [pltpu.make_async_copy(refs[i], refs[3 + i], sems.at[i]) for i in range(3)]
    for copy in copies:
        copy.start()
    for copy in copies:
        copy.wait()


def brought(after, place, *arrays):
    any_space = pl.BlockSpec(memory_space=pl.ANY)
    size = sum(v.size * 2 for v in arrays)
    return pl.pallas_call(
        bring,
        out_shape=[pltpu.VMEM(v.shape, v.dtype) for v in arrays],
        in_specs=[any_space, pl.BlockSpec(memory_space=pltpu.SMEM)] + [any_space] * 3,
        out_specs=[pl.BlockSpec(memory_space=pltpu.VMEM)] * 3,
        scratch_shapes=[pltpu.SemaphoreType.DMA((3,))],
        compiler_params=pltpu.CompilerParams(vmem_limit_bytes=1024 * 1024),
        cost_estimate=pl.CostEstimate(flops=0, bytes_accessed=2 * size, transcendentals=0),
    )(after, place, *[pltpu.with_memory_space_constraint(v, pltpu.HBM) for v in arrays])


def near_vmem(*arrays):
    return [pltpu.with_memory_space_constraint(v, pltpu.VMEM) for v in arrays]


def shares(place, starts, parts, hidden, frozen, head):
    rows, units = hidden.shape
    width = frozen.shape[1]
    any_space = pl.BlockSpec(memory_space=pl.ANY)
    smem = pl.BlockSpec(memory_space=pltpu.SMEM)
    vmem = pl.BlockSpec(memory_space=pltpu.VMEM)
    *outs, up_rest, grad_low, margin = pl.pallas_call(
        kernel,
        out_shape=[pltpu.VMEM((64, 16, LANES), BF)] * 2
        + [
            pltpu.VMEM((ORDER, width // 2), BF),
            pltpu.VMEM((ORDER, rows), BF),
            jax.ShapeDtypeStruct((8, 128), F32),
        ],
        in_specs=[smem, smem] + [any_space] * 16 + [vmem] * 3,
        out_specs=[vmem] * 5,
        scratch_shapes=[
            pltpu.VMEM((ORDER, units), BF),
            pltpu.VMEM((ORDER, width), BF),
            pltpu.VMEM((4, CHUNKS, 128), F32),
            pltpu.VMEM((CHUNKS, 128), F32),
            pltpu.VMEM((rows, width), F32),
            pltpu.VMEM((256, 16, LANES), BF),
            pltpu.SemaphoreType.DMA((16,)),
        ],
        compiler_params=pltpu.CompilerParams(vmem_limit_bytes=20 * 1024 * 1024),
        cost_estimate=pl.CostEstimate(
            flops=2 * rows * ORDER * (2 * units + 4 * width),
            bytes_accessed=2 * rows * (units + 2 * width) + 4 * 256 * 16 * LANES,
            transcendentals=0,
        ),
    )(place, starts, *parts, *near_vmem(hidden, frozen, head))
    rest = pl.pallas_call(
        second_kernel,
        out_shape=[pltpu.VMEM((64, 16, LANES), BF)] * 2,
        in_specs=[smem] + [vmem] * 3,
        out_specs=[vmem] * 2,
        scratch_shapes=[pltpu.VMEM((ORDER, (units // 256 + 1) * 128), BF)],
        compiler_params=pltpu.CompilerParams(vmem_limit_bytes=4 * 1024 * 1024),
        cost_estimate=pl.CostEstimate(
            flops=rows * ORDER * units,
            bytes_accessed=rows * units + 2 * 128 * 16 * LANES,
            transcendentals=0,
        ),
    )(place, *near_vmem(grad_low, up_rest, hidden))
    return outs, rest, margin[0, 0:1]


def device(z, y, x, c):
    return (((z * 2 + y // 2) * 4 + x) * 2 + y % 2) * 2 + c


def ring(values, step, turn=0):
    pairs = []
    for z, y, x, c in itertools.product(range(8), range(4), range(4), range(2)):
        along_y = c ^ turn
        to = device(z, (y + step * along_y) % 4, (x + step * (1 - along_y)) % 4, c)
        pairs.append((device(z, y, x, c), to))
    return lax.ppermute(values, FINE_AXES, pairs)


def other_core(values):
    return lax.ppermute(values, "c", [(0, 1), (1, 0)])


def total_of(*values):
    return sum(v.astype(F32) for v in values)


def local(
    gated_hidden_input,
    frozen,
    head_gradient_rows,
    down_factor_weight,
    up_factor_weight,
    final_norm_gain,
    logratio,
    starts,
):
    yl, core = lax.axis_index("yl"), lax.axis_index("c")
    place = jnp.stack([lax.axis_index("z"), lax.axis_index("yh") * 2 + yl, lax.axis_index("x"), core])

    quarter = packed(
        place,
        starts,
        logratio[0],
        down_factor_weight.T,
        up_factor_weight,
        final_norm_gain[None],
    )
    held = lax.all_to_all(quarter, "z", 0, 0, tiled=True)
    early = lax.optimization_barrier(
        (
            ring(held, 2),
            *[ring(held, step, 1) for step in (1, 2, 3)],
            ring(held, 1),
            ring(held, 3),
        )
    )
    side = jnp.concatenate(early[1:4])
    own = [held, side, early[4], ring(side, 1)]
    own += [early[0], ring(side, 2), early[5], ring(side, 3)]
    width = frozen.shape[3]
    near = brought(
        side,
        place,
        gated_hidden_input.reshape(-1, gated_hidden_input.shape[3]),
        frozen.reshape(-1, width),
        head_gradient_rows.reshape(-1, width),
    )
    small = [other_core(v) for v in own[::2]]
    side, *rest = lax.optimization_barrier((side, *near, *small))
    near, small = rest[:3], rest[3:]
    large = [other_core(v) for v in (side, *own[3::2])]
    other = [v for pair in zip(small, large) for v in pair]

    first, second, margin = shares(place, starts, [*own, *other], *near)

    lines = []
    for own, other in (first, second):
        came = other_core(other)
        chip = [
            total_of(own[16 * i : 16 * i + 16], came[16 * i : 16 * i + 16]).astype(BF)
            for i in range(4)
        ]
        came = [ring(chip[step], step) for step in (1, 2, 3)]
        lines.append(total_of(chip[0], *came).astype(BF).reshape(4, 4, 16, LANES))
    line = jnp.concatenate(lines, axis=1)
    came = [ring(line[step], step, 1) for step in (1, 2, 3)]
    plane = total_of(line[0], *came).astype(BF)
    share = jnp.sum(lax.all_to_all(plane, "z", 0, 0, tiled=True).astype(F32), axis=0)
    spread = [
        lax.ppermute(share, CTX, [(i, i ^ step) for i in range(4)]) for step in (2, 1, 3)
    ]
    down_gradient_t, up_gradient = finished(place, share, *spread)
    return jnp.logaddexp(0.0, -margin), down_gradient_t.T, up_gradient


def solution(mesh):
    fine = Mesh(mesh.devices.reshape(FINE_SHAPE), FINE_AXES)
    return jax.shard_map(
        local,
        mesh=fine,
        in_specs=(
            P(DP, None, CTX, None),
            P(DP, None, CTX, None),
            P(DP, None, CTX, None),
            P(DP, None),
            P(None, DP),
            P(DP),
            P(DP, None, CTX),
            P(DP, None),
        ),
        out_specs=(P(DP), P(DP, None), P(None, DP)),
        check_vma=False,
    )
```

```python
import itertools

import jax
import jax.numpy as jnp
from jax import lax
from jax.experimental import pallas as pl
from jax.experimental.pallas import tpu as pltpu
from jax.sharding import Mesh, PartitionSpec as P

SCALE = 2.0
BETA = 0.1
EPS = 1e-06

FINE_AXES = ("z", "yh", "x", "yl", "c")
FINE_SHAPE = (8, 2, 4, 2, 2)
DP = ("z", "yh", "x")
CTX = ("yl", "c")

LANES = 640
UP = 128
DOWN = 462
GAIN_AT = UP + DOWN
SUMS_AT = GAIN_AT + 32
CHUNKS = 64
ORDER = 64
BF, F32 = jnp.bfloat16, jnp.float32
NT = (((1,), (1,)), ((), ()))
NN = (((1,), (0,)), ((), ()))


def dot(a, b, dims):
    return lax.dot_general(a, b, dims, preferred_element_type=F32)


def slots(place, sign, planes):
    py, px, pc = place[1], place[2], place[3]
    dxs = [((sign * (px - x)) & 3) * planes for x in range(4)]
    dys = [((sign * (py - y)) & 3) * planes for y in range(4)]
    for x, yh, other, yl in itertools.product(range(4), range(2), range(2), range(2)):
        dx, dy = dxs[x], dys[yh * 2 + yl]
        yield x, yh, other, yl, jnp.where(pc == other, dx * 4 + dy, dy * 4 + dx)


def to_blocks(place, outs, first, up_share, grad_low, hid, held):
    origin = first * DOWN // 128 * 128
    stop = -(-(first + 32) * DOWN // 128) * 128
    for begin in range(origin, stop, 1024):
        end = min(begin + 1024, stop)
        held[:, begin - origin : end - origin] = dot(grad_low, hid[:, begin:end], NN).astype(BF)
    for x, yh, other, yl, base in slots(place, -1, 4):
        rows = slice(32 * other + 16 * yl, 32 * other + 16 * yl + 16)
        for z in range(4):
            chunk = z * 8 + yh * 4 + x
            begin = (first + chunk) * DOWN - origin
            outs[other][base + z, :, :UP] = up_share[rows, chunk * UP : chunk * UP + UP]
            outs[other][base + z, :, UP:GAIN_AT] = held[rows, begin : begin + DOWN]


def kernel(place_ref, starts_ref, *refs):
    parts, (hid, fro, hea) = refs[:8], refs[8:11]
    outs, up_rest, low_ref, margin_ref = refs[11:13], refs[13], refs[14], refs[15]
    wt, up, gains, gain, pol, block, sems = refs[16:]
    width = fro.shape[1]

    loads = [
        pltpu.make_async_copy(parts[i], block.at[pl.ds(32 * i, 32)], sems.at[i]) for i in range(8)
    ]
    for copy in loads:
        copy.start()
    for copy in loads:
        copy.wait()

    pz, py, px, pc = (place_ref[i] for i in range(4))
    sums = jnp.zeros((1, 128), F32)
    for other in range(2):
        for yl in range(2):
            y = (py & 2) + yl
            dy = (py - y) & 3
            inside = jnp.where(pc == other, dy * 8, dy * 32) + pz
            held = block[other * 128 + inside]
            sums += held[0:1, LANES - 128 :].astype(F32)
    lane = SUMS_AT - (LANES - 128)
    sides = [sum(sums[:, lane + 3 * s + j : lane + 3 * s + j + 1] for j in range(3)) for s in (0, 1)]
    margin = BETA * (sides[0] - sides[1])
    margin_ref[...] = jnp.broadcast_to(margin, margin_ref.shape)
    row = lax.broadcasted_iota(jnp.int32, (128, 1), 0)
    position = (row & 63) + ((py & 1) * 2 + pc) * 64
    start = jnp.where(row < 64, starts_ref[0, 0], starts_ref[0, 1])
    weight = jnp.where(row < 64, -BETA, BETA)
    slope = jnp.where(position >= start, weight, 0.0) / (1.0 + jnp.exp(margin))

    for x, yh, other, yl, base in slots(place_ref, 1, 8):
        q = other * 2 + yl
        rows = slice(16 * q, 16 * q + 16)
        for z in range(8):
            chunk = z * 8 + yh * 4 + x
            held = block[other * 128 + base + z]
            up[rows, chunk * UP : (chunk + 1) * UP] = held[:, :UP]
            wt[rows, chunk * DOWN : (chunk + 1) * DOWN] = held[:, UP:GAIN_AT]
            gains[q, chunk : chunk + 1, :] = held[0:1, LANES - 128 :].astype(F32)
    lane = GAIN_AT - (LANES - 128)
    parts_of_gain = [gains[q][:, lane : lane + 32] for q in range(4)]
    ordered = jnp.concatenate(parts_of_gain, axis=1)
    swapped = jnp.concatenate(parts_of_gain[2:] + parts_of_gain[:2], axis=1)
    gain[...] = jnp.where(pc == 0, ordered, swapped)

    tile = 5888
    main = wt.shape[1] // tile
    low = dot(hid[:, main * tile :], wt[:, main * tile :], NT)
    for i in range(main):
        at = slice(i * tile, i * tile + tile)
        low += dot(hid[:, at], wt[:, at], NT)
    low = low.astype(BF)
    low_t = low.astype(F32).T.astype(BF)

    step = 512

    def gained(i):
        pieces = []
        for j in range(step // 128):
            at = slice(i * step + j * 128, i * step + j * 128 + 128)
            chunk = i * (step // 128) + j
            pieces.append(hea[:, at].astype(F32) * gain[chunk : chunk + 1, :])
        return jnp.concatenate(pieces, axis=1)

    def fold(v):
        return sum(v[:, 128 * j : 128 * j + 128] for j in range(step // 128))

    def state_step(i, carry):
        squares, inner = carry
        at = slice(i * step, i * step + step)
        state = fro[:, at].astype(F32) + SCALE * dot(low, up[:, at], NN)
        pol[:, at] = state
        return squares + fold(state * state), inner + fold(gained(i) * state)

    zero = jnp.zeros((128, 128), F32)
    squares, inner = zero, zero
    for i in range(width // step):
        squares, inner = state_step(i, (squares, inner))
    rms = jnp.sqrt(jnp.sum(squares, axis=1, keepdims=True) / width + EPS)
    inner = slope * jnp.sum(inner, axis=1, keepdims=True)
    first = slope / rms
    second = inner / (width * rms * rms * rms)

    total = jnp.zeros((128, ORDER), F32)
    for i in range(width // step):
        at = slice(i * step, (i + 1) * step)
        grad = gained(i) * first - pol[:, at] * second
        high = grad.astype(BF)
        rest = (grad - high.astype(F32)).astype(BF)
        total += dot(high, up[:, at], NT) + dot(rest, up[:, at], NT)
        share = (SCALE * dot(low_t, high, NN)).astype(BF)
        if i * step < width // 2:
            up[:, at] = share
        else:
            up_rest[:, i * step - width // 2 : (i + 1) * step - width // 2] = share
    grad_low = (SCALE * total).T.astype(BF)

    low_ref[...] = grad_low
    to_blocks(place_ref, outs, 0, up, grad_low, hid, wt)


def second_kernel(place_ref, low_ref, up_rest, hid, *refs):
    to_blocks(place_ref, refs[:2], CHUNKS // 2, up_rest, low_ref[...], hid, refs[2])


def pack(place_ref, *refs):
    out_ref, sems = refs[5], refs[11]
    copies = [pltpu.make_async_copy(refs[i], refs[6 + i], sems.at[i]) for i in range(5)]
    for copy in copies:
        copy.start()
    for copy in copies:
        copy.wait()
    starts_ref, ratio_ref, down_ref, up_ref, gain_ref = refs[6:11]
    yl, core = place_ref[1] & 1, place_ref[3]
    begin = pl.multiple_of(core * 32 + yl * 16, 16)
    position = lax.broadcasted_iota(jnp.int32, (2, 64), 1) + (yl * 2 + core) * 64
    side = lax.broadcasted_iota(jnp.int32, (2, 64), 0)
    start = jnp.where(side == 0, starts_ref[0, 0], starts_ref[0, 1])
    total = jnp.sum(jnp.where(position >= start, ratio_ref[...], 0.0), axis=1, keepdims=True)
    high = total.astype(BF).astype(F32)
    middle = (total - high).astype(BF).astype(F32)
    low = total - high - middle

    lane = lax.broadcasted_iota(jnp.int32, (8, 128), 1)
    at = GAIN_AT - (LANES - 128)
    gain = jnp.broadcast_to(gain_ref[...].astype(F32), (8, 128))
    gain = pltpu.roll(gain, (at + 128 - (core * 2 + yl) * 32) & 127, 1)
    tail = jnp.where((lane >= at) & (lane < at + 32), gain, 0.0)
    for s in range(2):
        for j, part in enumerate((high, middle, low)):
            tail = jnp.where(lane == at + 32 + 3 * s + j, part[s : s + 1], tail)
    tail = jnp.concatenate([tail, tail], axis=0).astype(BF)
    rows = pl.ds(begin, 16)
    for i in range(8):
        out_ref[i, :, :UP] = up_ref[rows, :]
        out_ref[i, :, LANES - 128 :] = tail
        out_ref[i, :, UP:GAIN_AT] = down_ref[rows, :]


def packed(place, starts, *arrays):
    arrays = [starts, *arrays]
    return pl.pallas_call(
        pack,
        out_shape=jax.ShapeDtypeStruct((8, 16, LANES), BF),
        in_specs=[pl.BlockSpec(memory_space=pltpu.SMEM)]
        + [pl.BlockSpec(memory_space=pl.ANY)] * 5,
        out_specs=pl.BlockSpec(memory_space=pltpu.VMEM),
        scratch_shapes=[pltpu.SMEM(starts.shape, starts.dtype)]
        + [pltpu.VMEM(v.shape, v.dtype) for v in arrays[1:]]
        + [pltpu.SemaphoreType.DMA((5,))],
        compiler_params=pltpu.CompilerParams(vmem_limit_bytes=4 * 1024 * 1024),
    )(place, *[pltpu.with_memory_space_constraint(v, pltpu.HBM) for v in arrays])


def finish(place_ref, *refs):
    down_ref, up_ref = refs[4:]
    for i in range(4):
        core, yl = (place_ref[3] + i // 2) & 1, (place_ref[1] + i % 2) & 1
        rows = pl.ds(pl.multiple_of(core * 32 + yl * 16, 16), 16)
        up_ref[rows, :] = refs[i][:, :UP]
        down_ref[rows, :] = refs[i][:, UP:GAIN_AT]


def finished(place, *shares_):
    vmem = pl.BlockSpec(memory_space=pltpu.VMEM)
    return pl.pallas_call(
        finish,
        out_shape=[
            jax.ShapeDtypeStruct((ORDER, DOWN), F32),
            jax.ShapeDtypeStruct((ORDER, UP), F32),
        ],
        in_specs=[pl.BlockSpec(memory_space=pltpu.SMEM)] + [vmem] * 4,
        out_specs=[vmem] * 2,
        compiler_params=pltpu.CompilerParams(vmem_limit_bytes=4 * 1024 * 1024),
    )(place, *shares_)


def bring(after_ref, place_ref, *refs):
    sems = refs[6]
    copies = [pltpu.make_async_copy(refs[i], refs[3 + i], sems.at[i]) for i in range(3)]
    for copy in copies:
        copy.start()
    for copy in copies:
        copy.wait()


def brought(after, place, *arrays):
    any_space = pl.BlockSpec(memory_space=pl.ANY)
    size = sum(v.size * 2 for v in arrays)
    return pl.pallas_call(
        bring,
        out_shape=[pltpu.VMEM(v.shape, v.dtype) for v in arrays],
        in_specs=[any_space, pl.BlockSpec(memory_space=pltpu.SMEM)] + [any_space] * 3,
        out_specs=[pl.BlockSpec(memory_space=pltpu.VMEM)] * 3,
        scratch_shapes=[pltpu.SemaphoreType.DMA((3,))],
        compiler_params=pltpu.CompilerParams(vmem_limit_bytes=1024 * 1024),
        cost_estimate=pl.CostEstimate(flops=0, bytes_accessed=2 * size, transcendentals=0),
    )(after, place, *[pltpu.with_memory_space_constraint(v, pltpu.HBM) for v in arrays])


def near_vmem(*arrays):
    return [pltpu.with_memory_space_constraint(v, pltpu.VMEM) for v in arrays]


def shares(place, starts, parts, hidden, frozen, head):
    rows, units = hidden.shape
    width = frozen.shape[1]
    any_space = pl.BlockSpec(memory_space=pl.ANY)
    smem = pl.BlockSpec(memory_space=pltpu.SMEM)
    vmem = pl.BlockSpec(memory_space=pltpu.VMEM)
    *outs, up_rest, grad_low, margin = pl.pallas_call(
        kernel,
        out_shape=[pltpu.VMEM((64, 16, LANES), BF)] * 2
        + [
            pltpu.VMEM((ORDER, width // 2), BF),
            pltpu.VMEM((ORDER, rows), BF),
            jax.ShapeDtypeStruct((8, 128), F32),
        ],
        in_specs=[smem, smem] + [any_space] * 8 + [vmem] * 3,
        out_specs=[vmem] * 5,
        scratch_shapes=[
            pltpu.VMEM((ORDER, units), BF),
            pltpu.VMEM((ORDER, width), BF),
            pltpu.VMEM((4, CHUNKS, 128), F32),
            pltpu.VMEM((CHUNKS, 128), F32),
            pltpu.VMEM((rows, width), F32),
            pltpu.VMEM((256, 16, LANES), BF),
            pltpu.SemaphoreType.DMA((8,)),
        ],
        compiler_params=pltpu.CompilerParams(vmem_limit_bytes=20 * 1024 * 1024),
        cost_estimate=pl.CostEstimate(
            flops=2 * rows * ORDER * (2 * units + 4 * width),
            bytes_accessed=2 * rows * (units + 2 * width) + 4 * 256 * 16 * LANES,
            transcendentals=0,
        ),
    )(place, starts, *parts, *near_vmem(hidden, frozen, head))
    rest = pl.pallas_call(
        second_kernel,
        out_shape=[pltpu.VMEM((64, 16, LANES), BF)] * 2,
        in_specs=[smem] + [vmem] * 3,
        out_specs=[vmem] * 2,
        scratch_shapes=[pltpu.VMEM((ORDER, (units // 256 + 1) * 128), BF)],
        compiler_params=pltpu.CompilerParams(vmem_limit_bytes=4 * 1024 * 1024),
        cost_estimate=pl.CostEstimate(
            flops=rows * ORDER * units,
            bytes_accessed=rows * units + 2 * 128 * 16 * LANES,
            transcendentals=0,
        ),
    )(place, *near_vmem(grad_low, up_rest, hidden))
    return outs, rest, margin[0, 0:1]


def device(z, y, x, c):
    return (((z * 2 + y // 2) * 4 + x) * 2 + y % 2) * 2 + c


def ring(values, step, turn=0):
    pairs = []
    for z, y, x, c in itertools.product(range(8), range(4), range(4), range(2)):
        along_y = c ^ turn
        to = device(z, (y + step * along_y) % 4, (x + step * (1 - along_y)) % 4, c)
        pairs.append((device(z, y, x, c), to))
    return lax.ppermute(values, FINE_AXES, pairs)


def other_core(values):
    return lax.ppermute(values, "c", [(0, 1), (1, 0)])


def total_of(*values):
    return sum(v.astype(F32) for v in values)


def local(
    gated_hidden_input,
    frozen,
    head_gradient_rows,
    down_factor_weight,
    up_factor_weight,
    final_norm_gain,
    logratio,
    starts,
):
    yl, core = lax.axis_index("yl"), lax.axis_index("c")
    place = jnp.stack([lax.axis_index("z"), lax.axis_index("yh") * 2 + yl, lax.axis_index("x"), core])

    quarter = packed(
        place,
        starts,
        logratio[0],
        down_factor_weight.T,
        up_factor_weight,
        final_norm_gain[None],
    )
    held = lax.all_to_all(quarter, "z", 0, 0, tiled=True)
    line = jnp.concatenate([held] + [ring(held, step, 1) for step in (1, 2, 3)])
    own = [line] + [ring(line, step) for step in (1, 2, 3)]
    width = frozen.shape[3]
    near = brought(
        line,
        place,
        gated_hidden_input.reshape(-1, gated_hidden_input.shape[3]),
        frozen.reshape(-1, width),
        head_gradient_rows.reshape(-1, width),
    )
    line, *near = lax.optimization_barrier((line, *near))
    other = [other_core(v) for v in (line, *own[1:])]

    first, second, margin = shares(place, starts, [*own, *other], *near)

    lines = []
    for own, other in (first, second):
        came = other_core(other)
        chip = [
            total_of(own[16 * i : 16 * i + 16], came[16 * i : 16 * i + 16]).astype(BF)
            for i in range(4)
        ]
        came = [ring(chip[step], step) for step in (1, 2, 3)]
        lines.append(total_of(chip[0], *came).astype(BF).reshape(4, 4, 16, LANES))
    line = jnp.concatenate(lines, axis=1)
    came = [ring(line[step], step, 1) for step in (1, 2, 3)]
    plane = total_of(line[0], *came).astype(BF)
    share = jnp.sum(lax.all_to_all(plane, "z", 0, 0, tiled=True).astype(F32), axis=0)
    spread = [
        lax.ppermute(share, CTX, [(i, i ^ step) for i in range(4)]) for step in (2, 1, 3)
    ]
    down_gradient_t, up_gradient = finished(place, share, *spread)
    return jnp.logaddexp(0.0, -margin), down_gradient_t.T, up_gradient


def solution(mesh):
    fine = Mesh(mesh.devices.reshape(FINE_SHAPE), FINE_AXES)
    return jax.shard_map(
        local,
        mesh=fine,
        in_specs=(
            P(DP, None, CTX, None),
            P(DP, None, CTX, None),
            P(DP, None, CTX, None),
            P(DP, None),
            P(None, DP),
            P(DP),
            P(DP, None, CTX),
            P(DP, None),
        ),
        out_specs=(P(DP), P(DP, None), P(None, DP)),
        check_vma=False,
    )
```

```python
import itertools

import jax
import jax.numpy as jnp
from jax import lax
from jax.experimental import pallas as pl
from jax.experimental.pallas import tpu as pltpu
from jax.sharding import Mesh, PartitionSpec as P

SCALE = 2.0
BETA = 0.1
EPS = 1e-06

FINE_AXES = ("z", "yh", "x", "yl", "c")
FINE_SHAPE = (8, 2, 4, 2, 2)
DP = ("z", "yh", "x")
CTX = ("yl", "c")

LANES = 640
UP = 128
DOWN = 462
GAIN_AT = UP + DOWN
SUMS_AT = GAIN_AT + 32
CHUNKS = 64
ORDER = 64
BF, F32 = jnp.bfloat16, jnp.float32
NT = (((1,), (1,)), ((), ()))
NN = (((1,), (0,)), ((), ()))


def dot(a, b, dims):
    return lax.dot_general(a, b, dims, preferred_element_type=F32)


def slots(place, sign, planes, other):
    py, px, pc = place[1], place[2], place[3]
    dxs = [((sign * (px - x)) & 3) * planes for x in range(4)]
    dys = [((sign * (py - y)) & 3) * planes for y in range(4)]
    for x, yh, yl in itertools.product(range(4), range(2), range(2)):
        dx, dy = dxs[x], dys[yh * 2 + yl]
        yield x, yh, yl, jnp.where(pc == other, dx * 4 + dy, dy * 4 + dx)


def to_blocks(place, outs, first, up_share, grad_low, hid, held):
    origin = first * DOWN // 128 * 128
    stop = -(-(first + 32) * DOWN // 128) * 128
    for begin in range(origin, stop, 1024):
        end = min(begin + 1024, stop)
        held[:, begin - origin : end - origin] = dot(grad_low, hid[:, begin:end], NN).astype(BF)
    for other in range(2):
        for x, yh, yl, base in slots(place, -1, 4, other):
            rows = slice(32 * other + 16 * yl, 32 * other + 16 * yl + 16)
            for z in range(4):
                chunk = z * 8 + yh * 4 + x
                begin = (first + chunk) * DOWN - origin
                outs[other][base + z, :, :UP] = up_share[rows, chunk * UP : chunk * UP + UP]
                outs[other][base + z, :, UP:GAIN_AT] = held[rows, begin : begin + DOWN]


def kernel(place_ref, starts_ref, *refs):
    parts, (hid, fro, hea) = refs[:16], refs[16:19]
    outs, up_rest, low_ref, margin_ref = refs[19:21], refs[21], refs[22], refs[23]
    wt, up, gains, gain, pol, block, sems = refs[24:]
    width = fro.shape[1]

    loads = [
        pltpu.make_async_copy(parts[i], block.at[pl.ds(16 * i, 16)], sems.at[i]) for i in range(16)
    ]
    for copy in loads:
        copy.start()

    for other in range(2):
        for copy in loads[8 * other : 8 * other + 8]:
            copy.wait()
        for x, yh, yl, base in slots(place_ref, 1, 8, other):
            q = other * 2 + yl
            rows = slice(16 * q, 16 * q + 16)
            for z in range(8):
                chunk = z * 8 + yh * 4 + x
                held = block[other * 128 + base + z]
                up[rows, chunk * UP : (chunk + 1) * UP] = held[:, :UP]
                wt[rows, chunk * DOWN : (chunk + 1) * DOWN] = held[:, UP:GAIN_AT]
                gains[q, chunk : chunk + 1, :] = held[0:1, LANES - 128 :].astype(F32)

    pz, py, px, pc = (place_ref[i] for i in range(4))
    sums = jnp.zeros((1, 128), F32)
    for other in range(2):
        for yl in range(2):
            y = (py & 2) + yl
            dy = (py - y) & 3
            inside = jnp.where(pc == other, dy * 8, dy * 32) + pz
            held = block[other * 128 + inside]
            sums += held[0:1, LANES - 128 :].astype(F32)
    lane = SUMS_AT - (LANES - 128)
    sides = [sum(sums[:, lane + 3 * s + j : lane + 3 * s + j + 1] for j in range(3)) for s in (0, 1)]
    margin = BETA * (sides[0] - sides[1])
    margin_ref[...] = jnp.broadcast_to(margin, margin_ref.shape)
    row = lax.broadcasted_iota(jnp.int32, (128, 1), 0)
    position = (row & 63) + ((py & 1) * 2 + pc) * 64
    start = jnp.where(row < 64, starts_ref[0, 0], starts_ref[0, 1])
    weight = jnp.where(row < 64, -BETA, BETA)
    slope = jnp.where(position >= start, weight, 0.0) / (1.0 + jnp.exp(margin))

    lane = GAIN_AT - (LANES - 128)
    parts_of_gain = [gains[q][:, lane : lane + 32] for q in range(4)]
    ordered = jnp.concatenate(parts_of_gain, axis=1)
    swapped = jnp.concatenate(parts_of_gain[2:] + parts_of_gain[:2], axis=1)
    gain[...] = jnp.where(pc == 0, ordered, swapped)

    tile = 5888
    main = wt.shape[1] // tile
    low = dot(hid[:, main * tile :], wt[:, main * tile :], NT)
    for i in range(main):
        at = slice(i * tile, i * tile + tile)
        low += dot(hid[:, at], wt[:, at], NT)
    low = low.astype(BF)
    low_t = low.astype(F32).T.astype(BF)

    step = 512

    def gained(i):
        pieces = []
        for j in range(step // 128):
            at = slice(i * step + j * 128, i * step + j * 128 + 128)
            chunk = i * (step // 128) + j
            pieces.append(hea[:, at].astype(F32) * gain[chunk : chunk + 1, :])
        return jnp.concatenate(pieces, axis=1)

    def fold(v):
        return sum(v[:, 128 * j : 128 * j + 128] for j in range(step // 128))

    def state_step(i, carry):
        squares, inner = carry
        at = slice(i * step, i * step + step)
        state = fro[:, at].astype(F32) + SCALE * dot(low, up[:, at], NN)
        pol[:, at] = state
        return squares + fold(state * state), inner + fold(gained(i) * state)

    zero = jnp.zeros((128, 128), F32)
    squares, inner = zero, zero
    for i in range(width // step):
        squares, inner = state_step(i, (squares, inner))
    rms = jnp.sqrt(jnp.sum(squares, axis=1, keepdims=True) / width + EPS)
    inner = slope * jnp.sum(inner, axis=1, keepdims=True)
    first = slope / rms
    second = inner / (width * rms * rms * rms)

    total = jnp.zeros((128, ORDER), F32)
    for i in range(width // step):
        at = slice(i * step, (i + 1) * step)
        grad = gained(i) * first - pol[:, at] * second
        high = grad.astype(BF)
        rest = (grad - high.astype(F32)).astype(BF)
        total += dot(high, up[:, at], NT) + dot(rest, up[:, at], NT)
        share = (SCALE * dot(low_t, high, NN)).astype(BF)
        if i * step < width // 2:
            up[:, at] = share
        else:
            up_rest[:, i * step - width // 2 : (i + 1) * step - width // 2] = share
    grad_low = (SCALE * total).T.astype(BF)

    low_ref[...] = grad_low
    to_blocks(place_ref, outs, 0, up, grad_low, hid, wt)


def second_kernel(place_ref, low_ref, up_rest, hid, *refs):
    to_blocks(place_ref, refs[:2], CHUNKS // 2, up_rest, low_ref[...], hid, refs[2])


def pack(place_ref, *refs):
    out_ref, sems = refs[5], refs[11]
    copies = [pltpu.make_async_copy(refs[i], refs[6 + i], sems.at[i]) for i in range(5)]
    for copy in copies:
        copy.start()
    for copy in copies:
        copy.wait()
    starts_ref, ratio_ref, down_ref, up_ref, gain_ref = refs[6:11]
    yl, core = place_ref[1] & 1, place_ref[3]
    begin = pl.multiple_of(core * 32 + yl * 16, 16)
    position = lax.broadcasted_iota(jnp.int32, (2, 64), 1) + (yl * 2 + core) * 64
    side = lax.broadcasted_iota(jnp.int32, (2, 64), 0)
    start = jnp.where(side == 0, starts_ref[0, 0], starts_ref[0, 1])
    total = jnp.sum(jnp.where(position >= start, ratio_ref[...], 0.0), axis=1, keepdims=True)
    high = total.astype(BF).astype(F32)
    middle = (total - high).astype(BF).astype(F32)
    low = total - high - middle

    lane = lax.broadcasted_iota(jnp.int32, (8, 128), 1)
    at = GAIN_AT - (LANES - 128)
    gain = jnp.broadcast_to(gain_ref[...].astype(F32), (8, 128))
    gain = pltpu.roll(gain, (at + 128 - (core * 2 + yl) * 32) & 127, 1)
    tail = jnp.where((lane >= at) & (lane < at + 32), gain, 0.0)
    for s in range(2):
        for j, part in enumerate((high, middle, low)):
            tail = jnp.where(lane == at + 32 + 3 * s + j, part[s : s + 1], tail)
    tail = jnp.concatenate([tail, tail], axis=0).astype(BF)
    rows = pl.ds(begin, 16)
    for i in range(8):
        out_ref[i, :, :UP] = up_ref[rows, :]
        out_ref[i, :, LANES - 128 :] = tail
        out_ref[i, :, UP:GAIN_AT] = down_ref[rows, :]


def packed(place, starts, *arrays):
    arrays = [starts, *arrays]
    return pl.pallas_call(
        pack,
        out_shape=jax.ShapeDtypeStruct((8, 16, LANES), BF),
        in_specs=[pl.BlockSpec(memory_space=pltpu.SMEM)]
        + [pl.BlockSpec(memory_space=pl.ANY)] * 5,
        out_specs=pl.BlockSpec(memory_space=pltpu.VMEM),
        scratch_shapes=[pltpu.SMEM(starts.shape, starts.dtype)]
        + [pltpu.VMEM(v.shape, v.dtype) for v in arrays[1:]]
        + [pltpu.SemaphoreType.DMA((5,))],
        compiler_params=pltpu.CompilerParams(vmem_limit_bytes=4 * 1024 * 1024),
    )(place, *[pltpu.with_memory_space_constraint(v, pltpu.HBM) for v in arrays])


def finish(place_ref, *refs):
    down_ref, up_ref = refs[4:]
    for i in range(4):
        core, yl = (place_ref[3] + i // 2) & 1, (place_ref[1] + i % 2) & 1
        rows = pl.ds(pl.multiple_of(core * 32 + yl * 16, 16), 16)
        up_ref[rows, :] = refs[i][:, :UP]
        down_ref[rows, :] = refs[i][:, UP:GAIN_AT]


def finished(place, *shares_):
    vmem = pl.BlockSpec(memory_space=pltpu.VMEM)
    return pl.pallas_call(
        finish,
        out_shape=[
            jax.ShapeDtypeStruct((ORDER, DOWN), F32),
            jax.ShapeDtypeStruct((ORDER, UP), F32),
        ],
        in_specs=[pl.BlockSpec(memory_space=pltpu.SMEM)] + [vmem] * 4,
        out_specs=[vmem] * 2,
        compiler_params=pltpu.CompilerParams(vmem_limit_bytes=4 * 1024 * 1024),
    )(place, *shares_)


def bring(after_ref, place_ref, *refs):
    sems = refs[6]
    copies = [pltpu.make_async_copy(refs[i], refs[3 + i], sems.at[i]) for i in range(3)]
    for copy in copies:
        copy.start()
    for copy in copies:
        copy.wait()


def brought(after, place, *arrays):
    any_space = pl.BlockSpec(memory_space=pl.ANY)
    size = sum(v.size * 2 for v in arrays)
    return pl.pallas_call(
        bring,
        out_shape=[pltpu.VMEM(v.shape, v.dtype) for v in arrays],
        in_specs=[any_space, pl.BlockSpec(memory_space=pltpu.SMEM)] + [any_space] * 3,
        out_specs=[pl.BlockSpec(memory_space=pltpu.VMEM)] * 3,
        scratch_shapes=[pltpu.SemaphoreType.DMA((3,))],
        compiler_params=pltpu.CompilerParams(vmem_limit_bytes=1024 * 1024),
        cost_estimate=pl.CostEstimate(flops=0, bytes_accessed=2 * size, transcendentals=0),
    )(after, place, *[pltpu.with_memory_space_constraint(v, pltpu.HBM) for v in arrays])


def near_vmem(*arrays):
    return [pltpu.with_memory_space_constraint(v, pltpu.VMEM) for v in arrays]


def shares(place, starts, parts, hidden, frozen, head):
    rows, units = hidden.shape
    width = frozen.shape[1]
    any_space = pl.BlockSpec(memory_space=pl.ANY)
    smem = pl.BlockSpec(memory_space=pltpu.SMEM)
    vmem = pl.BlockSpec(memory_space=pltpu.VMEM)
    *outs, up_rest, grad_low, margin = pl.pallas_call(
        kernel,
        out_shape=[pltpu.VMEM((64, 16, LANES), BF)] * 2
        + [
            pltpu.VMEM((ORDER, width // 2), BF),
            pltpu.VMEM((ORDER, rows), BF),
            jax.ShapeDtypeStruct((8, 128), F32),
        ],
        in_specs=[smem, smem] + [any_space] * 16 + [vmem] * 3,
        out_specs=[vmem] * 5,
        scratch_shapes=[
            pltpu.VMEM((ORDER, units), BF),
            pltpu.VMEM((ORDER, width), BF),
            pltpu.VMEM((4, CHUNKS, 128), F32),
            pltpu.VMEM((CHUNKS, 128), F32),
            pltpu.VMEM((rows, width), F32),
            pltpu.VMEM((256, 16, LANES), BF),
            pltpu.SemaphoreType.DMA((16,)),
        ],
        compiler_params=pltpu.CompilerParams(vmem_limit_bytes=20 * 1024 * 1024),
        cost_estimate=pl.CostEstimate(
            flops=2 * rows * ORDER * (2 * units + 4 * width),
            bytes_accessed=2 * rows * (units + 2 * width) + 4 * 256 * 16 * LANES,
            transcendentals=0,
        ),
    )(place, starts, *parts, *near_vmem(hidden, frozen, head))
    rest = pl.pallas_call(
        second_kernel,
        out_shape=[pltpu.VMEM((64, 16, LANES), BF)] * 2,
        in_specs=[smem] + [vmem] * 3,
        out_specs=[vmem] * 2,
        scratch_shapes=[pltpu.VMEM((ORDER, (units // 256 + 1) * 128), BF)],
        compiler_params=pltpu.CompilerParams(vmem_limit_bytes=4 * 1024 * 1024),
        cost_estimate=pl.CostEstimate(
            flops=rows * ORDER * units,
            bytes_accessed=rows * units + 2 * 128 * 16 * LANES,
            transcendentals=0,
        ),
    )(place, *near_vmem(grad_low, up_rest, hidden))
    return outs, rest, margin[0, 0:1]


def device(z, y, x, c):
    return (((z * 2 + y // 2) * 4 + x) * 2 + y % 2) * 2 + c


def ring(values, step, turn=0):
    pairs = []
    for z, y, x, c in itertools.product(range(8), range(4), range(4), range(2)):
        along_y = c ^ turn
        to = device(z, (y + step * along_y) % 4, (x + step * (1 - along_y)) % 4, c)
        pairs.append((device(z, y, x, c), to))
    return lax.ppermute(values, FINE_AXES, pairs)


def other_core(values):
    return lax.ppermute(values, "c", [(0, 1), (1, 0)])


def total_of(*values):
    return sum(v.astype(F32) for v in values)


def local(
    gated_hidden_input,
    frozen,
    head_gradient_rows,
    down_factor_weight,
    up_factor_weight,
    final_norm_gain,
    logratio,
    starts,
):
    yl, core = lax.axis_index("yl"), lax.axis_index("c")
    place = jnp.stack([lax.axis_index("z"), lax.axis_index("yh") * 2 + yl, lax.axis_index("x"), core])

    quarter = packed(
        place,
        starts,
        logratio[0],
        down_factor_weight.T,
        up_factor_weight,
        final_norm_gain[None],
    )
    held = lax.all_to_all(quarter, "z", 0, 0, tiled=True)
    side = [ring(held, step, 1) for step in (1, 2, 3)]
    line = [jnp.concatenate([held, side[0]]), jnp.concatenate(side[1:])]
    behind = [ring(line[0], 1), ring(line[1], 1)]
    ahead = [ring(line[0], 3), ring(line[1], 3)]
    opposite = [ring(behind[0], 1), ring(ahead[1], 3)]
    width = frozen.shape[3]
    near = brought(
        line[1],
        place,
        gated_hidden_input.reshape(-1, gated_hidden_input.shape[3]),
        frozen.reshape(-1, width),
        head_gradient_rows.reshape(-1, width),
    )
    own = line + behind + opposite + ahead
    *early, near_0, near_1, near_2 = lax.optimization_barrier((*line, *behind, *ahead, *near))
    other = [other_core(v) for v in early[:4] + opposite + early[4:]]
    near = (near_0, near_1, near_2)

    first, second, margin = shares(place, starts, [*own, *other], *near)

    lines = []
    for (own, other), way in ((first, 1), (second, 3)):
        came = other_core(other)
        chip = [
            total_of(own[16 * i : 16 * i + 16], came[16 * i : 16 * i + 16]).astype(BF)
            for i in range(4)
        ]
        passing = ring(chip[2], way)
        direct = ring(chip[4 - way], 4 - way)
        joined = ring(total_of(chip[way], passing).astype(BF), way)
        lines.append(total_of(chip[0], direct, joined).astype(BF).reshape(4, 4, 16, LANES))
    line = jnp.concatenate(lines, axis=1)
    came = [ring(line[step], step, 1) for step in (1, 2, 3)]
    plane = total_of(line[0], *came).astype(BF)
    share = jnp.sum(lax.all_to_all(plane, "z", 0, 0, tiled=True).astype(F32), axis=0)
    spread = [
        lax.ppermute(share, CTX, [(i, i ^ step) for i in range(4)]) for step in (2, 1, 3)
    ]
    down_gradient_t, up_gradient = finished(place, share, *spread)
    return jnp.logaddexp(0.0, -margin), down_gradient_t.T, up_gradient


def solution(mesh):
    fine = Mesh(mesh.devices.reshape(FINE_SHAPE), FINE_AXES)
    return jax.shard_map(
        local,
        mesh=fine,
        in_specs=(
            P(DP, None, CTX, None),
            P(DP, None, CTX, None),
            P(DP, None, CTX, None),
            P(DP, None),
            P(None, DP),
            P(DP),
            P(DP, None, CTX),
            P(DP, None),
        ),
        out_specs=(P(DP), P(DP, None), P(None, DP)),
        check_vma=False,
    )
```

```python
import itertools

import jax
import jax.numpy as jnp
from jax import lax
from jax.experimental import pallas as pl
from jax.experimental.pallas import tpu as pltpu
from jax.sharding import Mesh, PartitionSpec as P

SCALE = 2.0
BETA = 0.1
EPS = 1e-06

FINE_AXES = ("z", "yh", "x", "yl", "c")
FINE_SHAPE = (8, 2, 4, 2, 2)
DP = ("z", "yh", "x")
CTX = ("yl", "c")

LANES = 640
UP = 128
DOWN = 462
GAIN_AT = UP + DOWN
SUMS_AT = GAIN_AT + 32
CHUNKS = 64
ORDER = 64
BF, F32 = jnp.bfloat16, jnp.float32
NT = (((1,), (1,)), ((), ()))
NN = (((1,), (0,)), ((), ()))


def dot(a, b, dims):
    return lax.dot_general(a, b, dims, preferred_element_type=F32)


def slots(place, sign, planes, other):
    py, px, pc = place[1], place[2], place[3]
    dxs = [((sign * (px - x)) & 3) * planes for x in range(4)]
    dys = [((sign * (py - y)) & 3) * planes for y in range(4)]
    for x, yh, yl in itertools.product(range(4), range(2), range(2)):
        dx, dy = dxs[x], dys[yh * 2 + yl]
        yield x, yh, yl, jnp.where(pc == other, dx * 4 + dy, dy * 4 + dx)


def to_blocks(place, outs, first, up_share, grad_low, hid, held):
    origin = first * DOWN // 128 * 128
    stop = -(-(first + 32) * DOWN // 128) * 128
    for begin in range(origin, stop, 1024):
        end = min(begin + 1024, stop)
        held[:, begin - origin : end - origin] = dot(grad_low, hid[:, begin:end], NN).astype(BF)
    for other in range(2):
        for x, yh, yl, base in slots(place, -1, 4, other):
            rows = slice(32 * other + 16 * yl, 32 * other + 16 * yl + 16)
            for z in range(4):
                chunk = z * 8 + yh * 4 + x
                begin = (first + chunk) * DOWN - origin
                outs[other][base + z, :, :UP] = up_share[rows, chunk * UP : chunk * UP + UP]
                outs[other][base + z, :, UP:GAIN_AT] = held[rows, begin : begin + DOWN]


def assemble(place_ref, other, parts, block, sems, hid, wt, up, gains):
    loads = [
        pltpu.make_async_copy(parts[i], block.at[pl.ds(16 * i, 16)], sems.at[i]) for i in range(8)
    ]
    for copy in loads:
        copy.start()
    for copy in loads:
        copy.wait()
    for x, yh, yl, base in slots(place_ref, 1, 8, other):
        rows = slice(16 * yl, 16 * yl + 16)
        for z in range(8):
            chunk = z * 8 + yh * 4 + x
            held = block[base + z]
            up[rows, chunk * UP : (chunk + 1) * UP] = held[:, :UP]
            wt[rows, chunk * DOWN : (chunk + 1) * DOWN] = held[:, UP:GAIN_AT]
            gains[yl, chunk : chunk + 1, :] = held[0:1, LANES - 128 :].astype(F32)

    pz, py, px, pc = (place_ref[i] for i in range(4))
    sums = jnp.zeros((1, 128), F32)
    for yl in range(2):
        dy = (py - ((py & 2) + yl)) & 3
        held = block[jnp.where(pc == other, dy * 8, dy * 32) + pz]
        sums += held[0:1, LANES - 128 :].astype(F32)

    tile = 5888
    main = wt.shape[1] // tile
    low = dot(hid[:, main * tile :], wt[:, main * tile :], NT)
    for i in range(main):
        at = slice(i * tile, i * tile + tile)
        low += dot(hid[:, at], wt[:, at], NT)
    return low, sums


def own_kernel(place_ref, *refs):
    parts, hid = refs[:8], refs[8]
    up, low_ref, gains, sums_ref = refs[9:13]
    block, wt, sems = refs[13:]
    low, sums = assemble(place_ref, 0, parts, block, sems, hid, wt, up, gains)
    low_ref[...] = low
    sums_ref[...] = jnp.broadcast_to(sums, sums_ref.shape)


def kernel(place_ref, starts_ref, *refs):
    parts, (hid, fro, hea) = refs[:8], refs[8:11]
    own_up, own_low, own_gains, own_sums = refs[11:15]
    outs, up_rest, low_ref, margin_ref = refs[15:17], refs[17], refs[18], refs[19]
    wt, up, gains, gain, pol, block, share_held, sems = refs[20:]
    width = fro.shape[1]

    up[:32, :] = own_up[...]
    low, sums = assemble(
        place_ref, 1, parts, block, sems, hid, wt, up.at[pl.ds(32, 32)], gains
    )
    low = jnp.concatenate([own_low[...], low], axis=1).astype(BF)
    low_t = low.astype(F32).T.astype(BF)

    py, pc = place_ref[1], place_ref[3]
    sums += own_sums[0:1, :]
    lane = SUMS_AT - (LANES - 128)
    sides = [sum(sums[:, lane + 3 * s + j : lane + 3 * s + j + 1] for j in range(3)) for s in (0, 1)]
    margin = BETA * (sides[0] - sides[1])
    margin_ref[...] = jnp.broadcast_to(margin, margin_ref.shape)
    row = lax.broadcasted_iota(jnp.int32, (128, 1), 0)
    position = (row & 63) + ((py & 1) * 2 + pc) * 64
    start = jnp.where(row < 64, starts_ref[0, 0], starts_ref[0, 1])
    weight = jnp.where(row < 64, -BETA, BETA)
    slope = jnp.where(position >= start, weight, 0.0) / (1.0 + jnp.exp(margin))

    lane = GAIN_AT - (LANES - 128)
    parts_of_gain = [v[:, lane : lane + 32] for v in (own_gains[0], own_gains[1], gains[0], gains[1])]
    ordered = jnp.concatenate(parts_of_gain, axis=1)
    swapped = jnp.concatenate(parts_of_gain[2:] + parts_of_gain[:2], axis=1)
    gain[...] = jnp.where(pc == 0, ordered, swapped)

    step = 512

    def gained(i):
        pieces = []
        for j in range(step // 128):
            at = slice(i * step + j * 128, i * step + j * 128 + 128)
            chunk = i * (step // 128) + j
            pieces.append(hea[:, at].astype(F32) * gain[chunk : chunk + 1, :])
        return jnp.concatenate(pieces, axis=1)

    def fold(v):
        return sum(v[:, 128 * j : 128 * j + 128] for j in range(step // 128))

    def state_step(i, carry):
        squares, inner = carry
        at = slice(i * step, i * step + step)
        state = fro[:, at].astype(F32) + SCALE * dot(low, up[:, at], NN)
        pol[:, at] = state
        return squares + fold(state * state), inner + fold(gained(i) * state)

    zero = jnp.zeros((128, 128), F32)
    squares, inner = zero, zero
    for i in range(width // step):
        squares, inner = state_step(i, (squares, inner))
    rms = jnp.sqrt(jnp.sum(squares, axis=1, keepdims=True) / width + EPS)
    inner = slope * jnp.sum(inner, axis=1, keepdims=True)
    first = slope / rms
    second = inner / (width * rms * rms * rms)

    total = jnp.zeros((128, ORDER), F32)
    for i in range(width // step):
        at = slice(i * step, (i + 1) * step)
        grad = gained(i) * first - pol[:, at] * second
        high = grad.astype(BF)
        rest = (grad - high.astype(F32)).astype(BF)
        total += dot(high, up[:, at], NT) + dot(rest, up[:, at], NT)
        share = (SCALE * dot(low_t, high, NN)).astype(BF)
        if i * step < width // 2:
            up[:, at] = share
        else:
            up_rest[:, i * step - width // 2 : (i + 1) * step - width // 2] = share
    grad_low = (SCALE * total).T.astype(BF)

    low_ref[...] = grad_low
    to_blocks(place_ref, outs, 0, up, grad_low, hid, share_held)


def second_kernel(place_ref, low_ref, up_rest, hid, *refs):
    to_blocks(place_ref, refs[:2], CHUNKS // 2, up_rest, low_ref[...], hid, refs[2])


def pack(place_ref, *refs):
    out_ref, sems = refs[5], refs[11]
    copies = [pltpu.make_async_copy(refs[i], refs[6 + i], sems.at[i]) for i in range(5)]
    for copy in copies:
        copy.start()
    for copy in copies:
        copy.wait()
    starts_ref, ratio_ref, down_ref, up_ref, gain_ref = refs[6:11]
    yl, core = place_ref[1] & 1, place_ref[3]
    begin = pl.multiple_of(core * 32 + yl * 16, 16)
    position = lax.broadcasted_iota(jnp.int32, (2, 64), 1) + (yl * 2 + core) * 64
    side = lax.broadcasted_iota(jnp.int32, (2, 64), 0)
    start = jnp.where(side == 0, starts_ref[0, 0], starts_ref[0, 1])
    total = jnp.sum(jnp.where(position >= start, ratio_ref[...], 0.0), axis=1, keepdims=True)
    high = total.astype(BF).astype(F32)
    middle = (total - high).astype(BF).astype(F32)
    low = total - high - middle

    lane = lax.broadcasted_iota(jnp.int32, (8, 128), 1)
    at = GAIN_AT - (LANES - 128)
    gain = jnp.broadcast_to(gain_ref[...].astype(F32), (8, 128))
    gain = pltpu.roll(gain, (at + 128 - (core * 2 + yl) * 32) & 127, 1)
    tail = jnp.where((lane >= at) & (lane < at + 32), gain, 0.0)
    for s in range(2):
        for j, part in enumerate((high, middle, low)):
            tail = jnp.where(lane == at + 32 + 3 * s + j, part[s : s + 1], tail)
    tail = jnp.concatenate([tail, tail], axis=0).astype(BF)
    rows = pl.ds(begin, 16)
    for i in range(8):
        out_ref[i, :, :UP] = up_ref[rows, :]
        out_ref[i, :, LANES - 128 :] = tail
        out_ref[i, :, UP:GAIN_AT] = down_ref[rows, :]


def packed(place, starts, *arrays):
    arrays = [starts, *arrays]
    return pl.pallas_call(
        pack,
        out_shape=jax.ShapeDtypeStruct((8, 16, LANES), BF),
        in_specs=[pl.BlockSpec(memory_space=pltpu.SMEM)]
        + [pl.BlockSpec(memory_space=pl.ANY)] * 5,
        out_specs=pl.BlockSpec(memory_space=pltpu.VMEM),
        scratch_shapes=[pltpu.SMEM(starts.shape, starts.dtype)]
        + [pltpu.VMEM(v.shape, v.dtype) for v in arrays[1:]]
        + [pltpu.SemaphoreType.DMA((5,))],
        compiler_params=pltpu.CompilerParams(vmem_limit_bytes=4 * 1024 * 1024),
    )(place, *[pltpu.with_memory_space_constraint(v, pltpu.HBM) for v in arrays])


def finish(place_ref, *refs):
    down_ref, up_ref = refs[4:]
    for i in range(4):
        core, yl = (place_ref[3] + i // 2) & 1, (place_ref[1] + i % 2) & 1
        rows = pl.ds(pl.multiple_of(core * 32 + yl * 16, 16), 16)
        up_ref[rows, :] = refs[i][:, :UP]
        down_ref[rows, :] = refs[i][:, UP:GAIN_AT]


def finished(place, *shares_):
    vmem = pl.BlockSpec(memory_space=pltpu.VMEM)
    return pl.pallas_call(
        finish,
        out_shape=[
            jax.ShapeDtypeStruct((ORDER, DOWN), F32),
            jax.ShapeDtypeStruct((ORDER, UP), F32),
        ],
        in_specs=[pl.BlockSpec(memory_space=pltpu.SMEM)] + [vmem] * 4,
        out_specs=[vmem] * 2,
        compiler_params=pltpu.CompilerParams(vmem_limit_bytes=4 * 1024 * 1024),
    )(place, *shares_)


def bring(after_ref, place_ref, *refs):
    sems = refs[6]
    copies = [pltpu.make_async_copy(refs[i], refs[3 + i], sems.at[i]) for i in range(3)]
    for copy in copies:
        copy.start()
    for copy in copies:
        copy.wait()


def brought(after, place, *arrays):
    any_space = pl.BlockSpec(memory_space=pl.ANY)
    size = sum(v.size * 2 for v in arrays)
    return pl.pallas_call(
        bring,
        out_shape=[pltpu.VMEM(v.shape, v.dtype) for v in arrays],
        in_specs=[any_space, pl.BlockSpec(memory_space=pltpu.SMEM)] + [any_space] * 3,
        out_specs=[pl.BlockSpec(memory_space=pltpu.VMEM)] * 3,
        scratch_shapes=[pltpu.SemaphoreType.DMA((3,))],
        compiler_params=pltpu.CompilerParams(vmem_limit_bytes=1024 * 1024),
        cost_estimate=pl.CostEstimate(flops=0, bytes_accessed=2 * size, transcendentals=0),
    )(after, place, *[pltpu.with_memory_space_constraint(v, pltpu.HBM) for v in arrays])


def near_vmem(*arrays):
    return [pltpu.with_memory_space_constraint(v, pltpu.VMEM) for v in arrays]


def shares(place, starts, own, other, hidden, frozen, head):
    rows, units = hidden.shape
    width = frozen.shape[1]
    any_space = pl.BlockSpec(memory_space=pl.ANY)
    smem = pl.BlockSpec(memory_space=pltpu.SMEM)
    vmem = pl.BlockSpec(memory_space=pltpu.VMEM)
    from_own = pl.pallas_call(
        own_kernel,
        out_shape=[
            pltpu.VMEM((ORDER // 2, width), BF),
            pltpu.VMEM((rows, ORDER // 2), F32),
            pltpu.VMEM((2, CHUNKS, 128), F32),
            pltpu.VMEM((8, 128), F32),
        ],
        in_specs=[smem] + [any_space] * 8 + [vmem],
        out_specs=[vmem] * 4,
        scratch_shapes=[
            pltpu.VMEM((128, 16, LANES), BF),
            pltpu.VMEM((ORDER // 2, units), BF),
            pltpu.SemaphoreType.DMA((8,)),
        ],
        compiler_params=pltpu.CompilerParams(vmem_limit_bytes=8 * 1024 * 1024),
        cost_estimate=pl.CostEstimate(
            flops=rows * ORDER * units,
            bytes_accessed=2 * rows * units + 4 * 128 * 16 * LANES,
            transcendentals=0,
        ),
    )(place, *own, *near_vmem(hidden))
    *outs, up_rest, grad_low, margin = pl.pallas_call(
        kernel,
        out_shape=[pltpu.VMEM((64, 16, LANES), BF)] * 2
        + [
            pltpu.VMEM((ORDER, width // 2), BF),
            pltpu.VMEM((ORDER, rows), BF),
            jax.ShapeDtypeStruct((8, 128), F32),
        ],
        in_specs=[smem, smem] + [any_space] * 8 + [vmem] * 7,
        out_specs=[vmem] * 5,
        scratch_shapes=[
            pltpu.VMEM((ORDER // 2, units), BF),
            pltpu.VMEM((ORDER, width), BF),
            pltpu.VMEM((2, CHUNKS, 128), F32),
            pltpu.VMEM((CHUNKS, 128), F32),
            pltpu.VMEM((rows, width), F32),
            pltpu.VMEM((128, 16, LANES), BF),
            pltpu.VMEM((ORDER, (units // 256 + 1) * 128), BF),
            pltpu.SemaphoreType.DMA((8,)),
        ],
        compiler_params=pltpu.CompilerParams(vmem_limit_bytes=18 * 1024 * 1024),
        cost_estimate=pl.CostEstimate(
            flops=2 * rows * ORDER * (2 * units + 4 * width),
            bytes_accessed=2 * rows * (units + 2 * width) + 4 * 256 * 16 * LANES,
            transcendentals=0,
        ),
    )(place, starts, *other, *near_vmem(hidden, frozen, head, *from_own))
    rest = pl.pallas_call(
        second_kernel,
        out_shape=[pltpu.VMEM((64, 16, LANES), BF)] * 2,
        in_specs=[smem] + [vmem] * 3,
        out_specs=[vmem] * 2,
        scratch_shapes=[pltpu.VMEM((ORDER, (units // 256 + 1) * 128), BF)],
        compiler_params=pltpu.CompilerParams(vmem_limit_bytes=4 * 1024 * 1024),
        cost_estimate=pl.CostEstimate(
            flops=rows * ORDER * units,
            bytes_accessed=rows * units + 2 * 128 * 16 * LANES,
            transcendentals=0,
        ),
    )(place, *near_vmem(grad_low, up_rest, hidden))
    return outs, rest, margin[0, 0:1]


def device(z, y, x, c):
    return (((z * 2 + y // 2) * 4 + x) * 2 + y % 2) * 2 + c


def ring(values, step, turn=0):
    pairs = []
    for z, y, x, c in itertools.product(range(8), range(4), range(4), range(2)):
        along_y = c ^ turn
        to = device(z, (y + step * along_y) % 4, (x + step * (1 - along_y)) % 4, c)
        pairs.append((device(z, y, x, c), to))
    return lax.ppermute(values, FINE_AXES, pairs)


def other_core(values):
    return lax.ppermute(values, "c", [(0, 1), (1, 0)])


def total_of(*values):
    return sum(v.astype(F32) for v in values)


def local(
    gated_hidden_input,
    frozen,
    head_gradient_rows,
    down_factor_weight,
    up_factor_weight,
    final_norm_gain,
    logratio,
    starts,
):
    yl, core = lax.axis_index("yl"), lax.axis_index("c")
    place = jnp.stack([lax.axis_index("z"), lax.axis_index("yh") * 2 + yl, lax.axis_index("x"), core])

    quarter = packed(
        place,
        starts,
        logratio[0],
        down_factor_weight.T,
        up_factor_weight,
        final_norm_gain[None],
    )
    held = lax.all_to_all(quarter, "z", 0, 0, tiled=True)
    side = [ring(held, step, 1) for step in (1, 2, 3)]
    line = [jnp.concatenate([held, side[0]]), jnp.concatenate(side[1:])]
    behind = [ring(line[0], 1), ring(line[1], 1)]
    ahead = [ring(line[0], 3), ring(line[1], 3)]
    opposite = [ring(behind[0], 1), ring(ahead[1], 3)]
    width = frozen.shape[3]
    near = brought(
        line[1],
        place,
        gated_hidden_input.reshape(-1, gated_hidden_input.shape[3]),
        frozen.reshape(-1, width),
        head_gradient_rows.reshape(-1, width),
    )
    own = line + behind + opposite + ahead
    *early, near_0, near_1, near_2 = lax.optimization_barrier((*line, *behind, *ahead, *near))
    other = [other_core(v) for v in early[:4] + opposite + early[4:]]
    near = (near_0, near_1, near_2)

    first, second, margin = shares(place, starts, own, other, *near)

    lines = []
    for own, other in (first, second):
        came = other_core(other)
        chip = [
            total_of(own[16 * i : 16 * i + 16], came[16 * i : 16 * i + 16]).astype(BF)
            for i in range(4)
        ]
        came = [ring(chip[step], step) for step in (1, 2, 3)]
        lines.append(total_of(chip[0], *came).astype(BF).reshape(4, 4, 16, LANES))
    line = jnp.concatenate(lines, axis=1)
    came = [ring(line[step], step, 1) for step in (1, 2, 3)]
    plane = total_of(line[0], *came).astype(BF)
    share = jnp.sum(lax.all_to_all(plane, "z", 0, 0, tiled=True).astype(F32), axis=0)
    spread = [
        lax.ppermute(share, CTX, [(i, i ^ step) for i in range(4)]) for step in (2, 1, 3)
    ]
    down_gradient_t, up_gradient = finished(place, share, *spread)
    return jnp.logaddexp(0.0, -margin), down_gradient_t.T, up_gradient


def solution(mesh):
    fine = Mesh(mesh.devices.reshape(FINE_SHAPE), FINE_AXES)
    return jax.shard_map(
        local,
        mesh=fine,
        in_specs=(
            P(DP, None, CTX, None),
            P(DP, None, CTX, None),
            P(DP, None, CTX, None),
            P(DP, None),
            P(None, DP),
            P(DP),
            P(DP, None, CTX),
            P(DP, None),
        ),
        out_specs=(P(DP), P(DP, None), P(None, DP)),
        check_vma=False,
    )
```

```python
import itertools

import jax
import jax.numpy as jnp
from jax import lax
from jax.experimental import pallas as pl
from jax.experimental.pallas import tpu as pltpu
from jax.sharding import Mesh, PartitionSpec as P

SCALE = 2.0
BETA = 0.1
EPS = 1e-06

FINE_AXES = ("z", "yh", "x", "yl", "c")
FINE_SHAPE = (8, 2, 4, 2, 2)
DP = ("z", "yh", "x")
CTX = ("yl", "c")

LANES = 640
UP = 128
DOWN = 462
GAIN_AT = UP + DOWN
SUMS_AT = GAIN_AT + 32
CHUNKS = 64
ORDER = 64
BF, F32 = jnp.bfloat16, jnp.float32
NT = (((1,), (1,)), ((), ()))
NN = (((1,), (0,)), ((), ()))


def dot(a, b, dims):
    return lax.dot_general(a, b, dims, preferred_element_type=F32)


def slots(place, sign, planes):
    py, px, pc = place[1], place[2], place[3]
    dxs = [((sign * (px - x)) & 3) * planes for x in range(4)]
    dys = [((sign * (py - y)) & 3) * planes for y in range(4)]
    for x, yh, other, yl in itertools.product(range(4), range(2), range(2), range(2)):
        dx, dy = dxs[x], dys[yh * 2 + yl]
        yield x, yh, other, yl, jnp.where(pc == other, dx * 4 + dy, dy * 4 + dx)


def to_blocks(place, outs, first, up_share, grad_low, hid, held):
    origin = first * DOWN // 128 * 128
    stop = -(-(first + 32) * DOWN // 128) * 128
    for begin in range(origin, stop, 1024):
        end = min(begin + 1024, stop)
        held[:, begin - origin : end - origin] = dot(grad_low, hid[:, begin:end], NN).astype(BF)
    for x, yh, other, yl, base in slots(place, -1, 4):
        rows = slice(32 * other + 16 * yl, 32 * other + 16 * yl + 16)
        for z in range(4):
            chunk = z * 8 + yh * 4 + x
            begin = (first + chunk) * DOWN - origin
            outs[other][base + z, :, :UP] = up_share[rows, chunk * UP : chunk * UP + UP]
            outs[other][base + z, :, UP:GAIN_AT] = held[rows, begin : begin + DOWN]


def kernel(place_ref, starts_ref, *refs):
    parts, (hid, fro, hea) = refs[:16], refs[16:19]
    outs, up_rest, low_ref, margin_ref = refs[19:21], refs[21], refs[22], refs[23]
    wt, up, gains, gain, pol, block, sems = refs[24:]
    width = fro.shape[1]

    loads = [
        pltpu.make_async_copy(parts[i], block.at[pl.ds(16 * i, 16)], sems.at[i]) for i in range(16)
    ]
    for copy in loads:
        copy.start()
    for copy in loads:
        copy.wait()

    pz, py, px, pc = (place_ref[i] for i in range(4))
    sums = jnp.zeros((1, 128), F32)
    for other in range(2):
        for yl in range(2):
            y = (py & 2) + yl
            dy = (py - y) & 3
            inside = jnp.where(pc == other, dy * 8, dy * 32) + pz
            held = block[other * 128 + inside]
            sums += held[0:1, LANES - 128 :].astype(F32)
    lane = SUMS_AT - (LANES - 128)
    sides = [sum(sums[:, lane + 3 * s + j : lane + 3 * s + j + 1] for j in range(3)) for s in (0, 1)]
    margin = BETA * (sides[0] - sides[1])
    margin_ref[...] = jnp.broadcast_to(margin, margin_ref.shape)
    row = lax.broadcasted_iota(jnp.int32, (128, 1), 0)
    position = (row & 63) + ((py & 1) * 2 + pc) * 64
    start = jnp.where(row < 64, starts_ref[0, 0], starts_ref[0, 1])
    weight = jnp.where(row < 64, -BETA, BETA)
    slope = jnp.where(position >= start, weight, 0.0) / (1.0 + jnp.exp(margin))

    for x, yh, other, yl, base in slots(place_ref, 1, 8):
        q = other * 2 + yl
        rows = slice(16 * q, 16 * q + 16)
        for z in range(8):
            chunk = z * 8 + yh * 4 + x
            held = block[other * 128 + base + z]
            up[rows, chunk * UP : (chunk + 1) * UP] = held[:, :UP]
            wt[rows, chunk * DOWN : (chunk + 1) * DOWN] = held[:, UP:GAIN_AT]
            gains[q, chunk : chunk + 1, :] = held[0:1, LANES - 128 :].astype(F32)
    lane = GAIN_AT - (LANES - 128)
    parts_of_gain = [gains[q][:, lane : lane + 32] for q in range(4)]
    ordered = jnp.concatenate(parts_of_gain, axis=1)
    swapped = jnp.concatenate(parts_of_gain[2:] + parts_of_gain[:2], axis=1)
    gain[...] = jnp.where(pc == 0, ordered, swapped)

    tile = 5888
    main = wt.shape[1] // tile
    low = dot(hid[:, main * tile :], wt[:, main * tile :], NT)
    for i in range(main):
        at = slice(i * tile, i * tile + tile)
        low += dot(hid[:, at], wt[:, at], NT)
    low = low.astype(BF)
    low_t = low.astype(F32).T.astype(BF)

    step = 512

    def gained(i):
        pieces = []
        for j in range(step // 128):
            at = slice(i * step + j * 128, i * step + j * 128 + 128)
            chunk = i * (step // 128) + j
            pieces.append(hea[:, at].astype(F32) * gain[chunk : chunk + 1, :])
        return jnp.concatenate(pieces, axis=1)

    def fold(v):
        return sum(v[:, 128 * j : 128 * j + 128] for j in range(step // 128))

    def state_step(i, carry):
        squares, inner = carry
        at = slice(i * step, i * step + step)
        state = fro[:, at].astype(F32) + SCALE * dot(low, up[:, at], NN)
        pol[:, at] = state
        return squares + fold(state * state), inner + fold(gained(i) * state)

    zero = jnp.zeros((128, 128), F32)
    squares, inner = zero, zero
    for i in range(width // step):
        squares, inner = state_step(i, (squares, inner))
    rms = jnp.sqrt(jnp.sum(squares, axis=1, keepdims=True) / width + EPS)
    inner = slope * jnp.sum(inner, axis=1, keepdims=True)
    first = slope / rms
    second = inner / (width * rms * rms * rms)

    total = jnp.zeros((128, ORDER), F32)
    for i in range(width // step):
        at = slice(i * step, (i + 1) * step)
        grad = gained(i) * first - pol[:, at] * second
        high = grad.astype(BF)
        rest = (grad - high.astype(F32)).astype(BF)
        total += dot(high, up[:, at], NT) + dot(rest, up[:, at], NT)
        share = (SCALE * dot(low_t, high, NN)).astype(BF)
        if i * step < width // 2:
            up[:, at] = share
        else:
            up_rest[:, i * step - width // 2 : (i + 1) * step - width // 2] = share
    grad_low = (SCALE * total).T.astype(BF)

    low_ref[...] = grad_low
    to_blocks(place_ref, outs, 0, up, grad_low, hid, wt)


def second_kernel(place_ref, low_ref, up_rest, hid, *refs):
    to_blocks(place_ref, refs[:2], CHUNKS // 2, up_rest, low_ref[...], hid, refs[2])


def pack(place_ref, *refs):
    out_ref, sems = refs[5], refs[11]
    copies = [pltpu.make_async_copy(refs[i], refs[6 + i], sems.at[i]) for i in range(5)]
    for copy in copies:
        copy.start()
    for copy in copies:
        copy.wait()
    starts_ref, ratio_ref, down_ref, up_ref, gain_ref = refs[6:11]
    yl, core = place_ref[1] & 1, place_ref[3]
    begin = pl.multiple_of(core * 32 + yl * 16, 16)
    position = lax.broadcasted_iota(jnp.int32, (2, 64), 1) + (yl * 2 + core) * 64
    side = lax.broadcasted_iota(jnp.int32, (2, 64), 0)
    start = jnp.where(side == 0, starts_ref[0, 0], starts_ref[0, 1])
    total = jnp.sum(jnp.where(position >= start, ratio_ref[...], 0.0), axis=1, keepdims=True)
    high = total.astype(BF).astype(F32)
    middle = (total - high).astype(BF).astype(F32)
    low = total - high - middle

    lane = lax.broadcasted_iota(jnp.int32, (8, 128), 1)
    at = GAIN_AT - (LANES - 128)
    gain = jnp.broadcast_to(gain_ref[...].astype(F32), (8, 128))
    gain = pltpu.roll(gain, (at + 128 - (core * 2 + yl) * 32) & 127, 1)
    tail = jnp.where((lane >= at) & (lane < at + 32), gain, 0.0)
    for s in range(2):
        for j, part in enumerate((high, middle, low)):
            tail = jnp.where(lane == at + 32 + 3 * s + j, part[s : s + 1], tail)
    tail = jnp.concatenate([tail, tail], axis=0).astype(BF)
    rows = pl.ds(begin, 16)
    for i in range(8):
        out_ref[i, :, :UP] = up_ref[rows, :]
        out_ref[i, :, LANES - 128 :] = tail
        out_ref[i, :, UP:GAIN_AT] = down_ref[rows, :]


def packed(place, starts, *arrays):
    arrays = [starts, *arrays]
    return pl.pallas_call(
        pack,
        out_shape=pltpu.VMEM((8, 16, LANES), BF),
        in_specs=[pl.BlockSpec(memory_space=pltpu.SMEM)]
        + [pl.BlockSpec(memory_space=pl.ANY)] * 5,
        out_specs=pl.BlockSpec(memory_space=pltpu.VMEM),
        scratch_shapes=[pltpu.SMEM(starts.shape, starts.dtype)]
        + [pltpu.VMEM(v.shape, v.dtype) for v in arrays[1:]]
        + [pltpu.SemaphoreType.DMA((5,))],
        compiler_params=pltpu.CompilerParams(vmem_limit_bytes=4 * 1024 * 1024),
    )(place, *[pltpu.with_memory_space_constraint(v, pltpu.HBM) for v in arrays])


def finish(place_ref, *refs):
    down_ref, up_ref = refs[4:]
    for i in range(4):
        core, yl = (place_ref[3] + i // 2) & 1, (place_ref[1] + i % 2) & 1
        rows = pl.ds(pl.multiple_of(core * 32 + yl * 16, 16), 16)
        up_ref[rows, :] = refs[i][:, :UP]
        down_ref[rows, :] = refs[i][:, UP:GAIN_AT]


def finished(place, *shares_):
    vmem = pl.BlockSpec(memory_space=pltpu.VMEM)
    return pl.pallas_call(
        finish,
        out_shape=[
            jax.ShapeDtypeStruct((ORDER, DOWN), F32),
            jax.ShapeDtypeStruct((ORDER, UP), F32),
        ],
        in_specs=[pl.BlockSpec(memory_space=pltpu.SMEM)] + [vmem] * 4,
        out_specs=[vmem] * 2,
        compiler_params=pltpu.CompilerParams(vmem_limit_bytes=4 * 1024 * 1024),
    )(place, *near_vmem(*shares_))


def bring(after_ref, place_ref, *refs):
    sems = refs[6]
    copies = [pltpu.make_async_copy(refs[i], refs[3 + i], sems.at[i]) for i in range(3)]
    for copy in copies:
        copy.start()
    for copy in copies:
        copy.wait()


def brought(after, place, *arrays):
    any_space = pl.BlockSpec(memory_space=pl.ANY)
    size = sum(v.size * 2 for v in arrays)
    return pl.pallas_call(
        bring,
        out_shape=[pltpu.VMEM(v.shape, v.dtype) for v in arrays],
        in_specs=[any_space, pl.BlockSpec(memory_space=pltpu.SMEM)] + [any_space] * 3,
        out_specs=[pl.BlockSpec(memory_space=pltpu.VMEM)] * 3,
        scratch_shapes=[pltpu.SemaphoreType.DMA((3,))],
        compiler_params=pltpu.CompilerParams(vmem_limit_bytes=1024 * 1024),
        cost_estimate=pl.CostEstimate(flops=0, bytes_accessed=2 * size, transcendentals=0),
    )(after, place, *[pltpu.with_memory_space_constraint(v, pltpu.HBM) for v in arrays])


def near_vmem(*arrays):
    return [pltpu.with_memory_space_constraint(v, pltpu.VMEM) for v in arrays]


def shares(place, starts, parts, hidden, frozen, head):
    rows, units = hidden.shape
    width = frozen.shape[1]
    any_space = pl.BlockSpec(memory_space=pl.ANY)
    smem = pl.BlockSpec(memory_space=pltpu.SMEM)
    vmem = pl.BlockSpec(memory_space=pltpu.VMEM)
    *outs, up_rest, grad_low, margin = pl.pallas_call(
        kernel,
        out_shape=[pltpu.VMEM((64, 16, LANES), BF)] * 2
        + [
            pltpu.VMEM((ORDER, width // 2), BF),
            pltpu.VMEM((ORDER, rows), BF),
            jax.ShapeDtypeStruct((8, 128), F32),
        ],
        in_specs=[smem, smem] + [any_space] * 16 + [vmem] * 3,
        out_specs=[vmem] * 5,
        scratch_shapes=[
            pltpu.VMEM((ORDER, units), BF),
            pltpu.VMEM((ORDER, width), BF),
            pltpu.VMEM((4, CHUNKS, 128), F32),
            pltpu.VMEM((CHUNKS, 128), F32),
            pltpu.VMEM((rows, width), F32),
            pltpu.VMEM((256, 16, LANES), BF),
            pltpu.SemaphoreType.DMA((16,)),
        ],
        compiler_params=pltpu.CompilerParams(vmem_limit_bytes=20 * 1024 * 1024),
        cost_estimate=pl.CostEstimate(
            flops=2 * rows * ORDER * (2 * units + 4 * width),
            bytes_accessed=2 * rows * (units + 2 * width) + 4 * 256 * 16 * LANES,
            transcendentals=0,
        ),
    )(place, starts, *parts, *near_vmem(hidden, frozen, head))
    rest = pl.pallas_call(
        second_kernel,
        out_shape=[pltpu.VMEM((64, 16, LANES), BF)] * 2,
        in_specs=[smem] + [vmem] * 3,
        out_specs=[vmem] * 2,
        scratch_shapes=[pltpu.VMEM((ORDER, (units // 256 + 1) * 128), BF)],
        compiler_params=pltpu.CompilerParams(vmem_limit_bytes=4 * 1024 * 1024),
        cost_estimate=pl.CostEstimate(
            flops=rows * ORDER * units,
            bytes_accessed=rows * units + 2 * 128 * 16 * LANES,
            transcendentals=0,
        ),
    )(place, *near_vmem(grad_low, up_rest, hidden))
    return outs, rest, margin[0, 0:1]


def device(z, y, x, c):
    return (((z * 2 + y // 2) * 4 + x) * 2 + y % 2) * 2 + c


def ring(values, step, turn=0):
    pairs = []
    for z, y, x, c in itertools.product(range(8), range(4), range(4), range(2)):
        along_y = c ^ turn
        to = device(z, (y + step * along_y) % 4, (x + step * (1 - along_y)) % 4, c)
        pairs.append((device(z, y, x, c), to))
    return lax.ppermute(values, FINE_AXES, pairs)


def other_core(values):
    return lax.ppermute(values, "c", [(0, 1), (1, 0)])


def total_of(*values):
    return sum(v.astype(F32) for v in values)


def local(
    gated_hidden_input,
    frozen,
    head_gradient_rows,
    down_factor_weight,
    up_factor_weight,
    final_norm_gain,
    logratio,
    starts,
):
    yl, core = lax.axis_index("yl"), lax.axis_index("c")
    place = jnp.stack([lax.axis_index("z"), lax.axis_index("yh") * 2 + yl, lax.axis_index("x"), core])

    quarter = packed(
        place,
        starts,
        logratio[0],
        down_factor_weight.T,
        up_factor_weight,
        final_norm_gain[None],
    )
    held = lax.all_to_all(quarter, "z", 0, 0, tiled=True)
    side = [ring(held, step, 1) for step in (1, 2, 3)]
    line = [jnp.concatenate([held, side[0]]), jnp.concatenate(side[1:])]
    behind = [ring(line[0], 1), ring(line[1], 1)]
    ahead = [ring(line[0], 3), ring(line[1], 3)]
    opposite = [ring(behind[0], 1), ring(ahead[1], 3)]
    width = frozen.shape[3]
    near = brought(
        line[1],
        place,
        gated_hidden_input.reshape(-1, gated_hidden_input.shape[3]),
        frozen.reshape(-1, width),
        head_gradient_rows.reshape(-1, width),
    )
    own = line + behind + opposite + ahead
    *early, near_0, near_1, near_2 = lax.optimization_barrier((*line, *behind, *ahead, *near))
    other = [other_core(v) for v in early[:4] + opposite + early[4:]]
    near = (near_0, near_1, near_2)

    first, second, margin = shares(place, starts, [*own, *other], *near)

    lines = []
    for own, other in (first, second):
        came = other_core(other)
        chip = [
            total_of(own[16 * i : 16 * i + 16], came[16 * i : 16 * i + 16]).astype(BF)
            for i in range(4)
        ]
        came = [ring(chip[step], step) for step in (1, 2, 3)]
        lines.append(total_of(chip[0], *came).astype(BF).reshape(4, 4, 16, LANES))
    line = jnp.concatenate(lines, axis=1)
    came = [ring(line[step], step, 1) for step in (1, 2, 3)]
    plane = total_of(line[0], *came).astype(BF)
    share = jnp.sum(lax.all_to_all(plane, "z", 0, 0, tiled=True).astype(F32), axis=0)
    spread = [
        lax.ppermute(share, CTX, [(i, i ^ step) for i in range(4)]) for step in (2, 1, 3)
    ]
    down_gradient_t, up_gradient = finished(place, share, *spread)
    return jnp.logaddexp(0.0, -margin), down_gradient_t.T, up_gradient


def solution(mesh):
    fine = Mesh(mesh.devices.reshape(FINE_SHAPE), FINE_AXES)
    return jax.shard_map(
        local,
        mesh=fine,
        in_specs=(
            P(DP, None, CTX, None),
            P(DP, None, CTX, None),
            P(DP, None, CTX, None),
            P(DP, None),
            P(None, DP),
            P(DP),
            P(DP, None, CTX),
            P(DP, None),
        ),
        out_specs=(P(DP), P(DP, None), P(None, DP)),
        check_vma=False,
    )
```

```python
import itertools

import jax
import jax.numpy as jnp
from jax import lax
from jax.experimental import pallas as pl
from jax.experimental.pallas import tpu as pltpu
from jax.sharding import Mesh, PartitionSpec as P

SCALE = 2.0
BETA = 0.1
EPS = 1e-06

FINE_AXES = ("z", "yh", "x", "yl", "c")
FINE_SHAPE = (8, 2, 4, 2, 2)
DP = ("z", "yh", "x")
CTX = ("yl", "c")

LANES = 640
UP = 128
DOWN = 462
GAIN_AT = UP + DOWN
SUMS_AT = GAIN_AT + 32
CHUNKS = 64
ORDER = 64
PLANES = 3
BF, F32 = jnp.bfloat16, jnp.float32
NT = (((1,), (1,)), ((), ()))
NN = (((1,), (0,)), ((), ()))


def dot(a, b, dims):
    return lax.dot_general(a, b, dims, preferred_element_type=F32)


def slots(place, sign, planes):
    py, px, pc = place[1], place[2], place[3]
    dxs = [((sign * (px - x)) & 3) * planes for x in range(4)]
    dys = [((sign * (py - y)) & 3) * planes for y in range(4)]
    for x, yh, other, yl in itertools.product(range(4), range(2), range(2), range(2)):
        dx, dy = dxs[x], dys[yh * 2 + yl]
        yield x, yh, other, yl, jnp.where(pc == other, dx * 4 + dy, dy * 4 + dx)


def to_blocks(place, outs, first, planes, up_share, grad_low, hid, held):
    origin = first * DOWN // 128 * 128
    stop = -(-(first + 8 * planes) * DOWN // 128) * 128
    for begin in range(origin, stop, 1024):
        end = min(begin + 1024, stop)
        held[:, begin - origin : end - origin] = dot(grad_low, hid[:, begin:end], NN).astype(BF)
    for x, yh, other, yl, base in slots(place, -1, planes):
        rows = slice(32 * other + 16 * yl, 32 * other + 16 * yl + 16)
        for z in range(planes):
            chunk = z * 8 + yh * 4 + x
            begin = (first + chunk) * DOWN - origin
            outs[other][base + z, :, :UP] = up_share[rows, chunk * UP : chunk * UP + UP]
            outs[other][base + z, :, UP:GAIN_AT] = held[rows, begin : begin + DOWN]


def kernel(place_ref, starts_ref, *refs):
    parts, (hid, fro, hea) = refs[:8], refs[8:11]
    outs, up_rest, low_ref, margin_ref = refs[11:13], refs[13], refs[14], refs[15]
    wt, up, gains, gain, pol, block, sems = refs[16:]
    width = fro.shape[1]

    loads = [
        pltpu.make_async_copy(parts[i], block.at[pl.ds(32 * i, 32)], sems.at[i]) for i in range(8)
    ]
    for copy in loads:
        copy.start()
    for copy in loads:
        copy.wait()

    pz, py, px, pc = (place_ref[i] for i in range(4))
    sums = jnp.zeros((1, 128), F32)
    for other in range(2):
        for yl in range(2):
            y = (py & 2) + yl
            dy = (py - y) & 3
            inside = jnp.where(pc == other, dy * 8, dy * 32) + pz
            held = block[other * 128 + inside]
            sums += held[0:1, LANES - 128 :].astype(F32)
    lane = SUMS_AT - (LANES - 128)
    sides = [sum(sums[:, lane + 3 * s + j : lane + 3 * s + j + 1] for j in range(3)) for s in (0, 1)]
    margin = BETA * (sides[0] - sides[1])
    margin_ref[...] = jnp.broadcast_to(margin, margin_ref.shape)
    row = lax.broadcasted_iota(jnp.int32, (128, 1), 0)
    position = (row & 63) + ((py & 1) * 2 + pc) * 64
    start = jnp.where(row < 64, starts_ref[0, 0], starts_ref[0, 1])
    weight = jnp.where(row < 64, -BETA, BETA)
    slope = jnp.where(position >= start, weight, 0.0) / (1.0 + jnp.exp(margin))

    for x, yh, other, yl, base in slots(place_ref, 1, 8):
        q = other * 2 + yl
        rows = slice(16 * q, 16 * q + 16)
        for z in range(8):
            chunk = z * 8 + yh * 4 + x
            held = block[other * 128 + base + z]
            up[rows, chunk * UP : (chunk + 1) * UP] = held[:, :UP]
            wt[rows, chunk * DOWN : (chunk + 1) * DOWN] = held[:, UP:GAIN_AT]
            gains[q, chunk : chunk + 1, :] = held[0:1, LANES - 128 :].astype(F32)
    lane = GAIN_AT - (LANES - 128)
    parts_of_gain = [gains[q][:, lane : lane + 32] for q in range(4)]
    ordered = jnp.concatenate(parts_of_gain, axis=1)
    swapped = jnp.concatenate(parts_of_gain[2:] + parts_of_gain[:2], axis=1)
    gain[...] = jnp.where(pc == 0, ordered, swapped)

    tile = 5888
    main = wt.shape[1] // tile
    low = dot(hid[:, main * tile :], wt[:, main * tile :], NT)
    for i in range(main):
        at = slice(i * tile, i * tile + tile)
        low += dot(hid[:, at], wt[:, at], NT)
    low = low.astype(BF)
    low_t = low.astype(F32).T.astype(BF)

    step = 512

    def gained(i):
        pieces = []
        for j in range(step // 128):
            at = slice(i * step + j * 128, i * step + j * 128 + 128)
            chunk = i * (step // 128) + j
            pieces.append(hea[:, at].astype(F32) * gain[chunk : chunk + 1, :])
        return jnp.concatenate(pieces, axis=1)

    def fold(v):
        return sum(v[:, 128 * j : 128 * j + 128] for j in range(step // 128))

    def state_step(i, carry):
        squares, inner = carry
        at = slice(i * step, i * step + step)
        state = fro[:, at].astype(F32) + SCALE * dot(low, up[:, at], NN)
        pol[:, at] = state
        return squares + fold(state * state), inner + fold(gained(i) * state)

    zero = jnp.zeros((128, 128), F32)
    squares, inner = zero, zero
    for i in range(width // step):
        squares, inner = state_step(i, (squares, inner))
    rms = jnp.sqrt(jnp.sum(squares, axis=1, keepdims=True) / width + EPS)
    inner = slope * jnp.sum(inner, axis=1, keepdims=True)
    first = slope / rms
    second = inner / (width * rms * rms * rms)

    packed_here = PLANES * 8 * UP
    total = jnp.zeros((128, ORDER), F32)
    for i in range(width // step):
        at = slice(i * step, (i + 1) * step)
        grad = gained(i) * first - pol[:, at] * second
        high = grad.astype(BF)
        rest = (grad - high.astype(F32)).astype(BF)
        total += dot(high, up[:, at], NT) + dot(rest, up[:, at], NT)
        share = (SCALE * dot(low_t, high, NN)).astype(BF)
        if i * step < packed_here:
            up[:, at] = share
        else:
            up_rest[:, i * step - packed_here : (i + 1) * step - packed_here] = share
    grad_low = (SCALE * total).T.astype(BF)

    low_ref[...] = grad_low
    to_blocks(place_ref, outs, 0, PLANES, up, grad_low, hid, wt)


def second_kernel(place_ref, low_ref, up_rest, hid, *refs):
    to_blocks(
        place_ref, refs[:2], 8 * PLANES, 8 - PLANES, up_rest, low_ref[...], hid, refs[2]
    )


def pack(place_ref, *refs):
    out_ref, sems = refs[5], refs[11]
    copies = [pltpu.make_async_copy(refs[i], refs[6 + i], sems.at[i]) for i in range(5)]
    for copy in copies:
        copy.start()
    for copy in copies:
        copy.wait()
    starts_ref, ratio_ref, down_ref, up_ref, gain_ref = refs[6:11]
    yl, core = place_ref[1] & 1, place_ref[3]
    begin = pl.multiple_of(core * 32 + yl * 16, 16)
    position = lax.broadcasted_iota(jnp.int32, (2, 64), 1) + (yl * 2 + core) * 64
    side = lax.broadcasted_iota(jnp.int32, (2, 64), 0)
    start = jnp.where(side == 0, starts_ref[0, 0], starts_ref[0, 1])
    total = jnp.sum(jnp.where(position >= start, ratio_ref[...], 0.0), axis=1, keepdims=True)
    high = total.astype(BF).astype(F32)
    middle = (total - high).astype(BF).astype(F32)
    low = total - high - middle

    lane = lax.broadcasted_iota(jnp.int32, (8, 128), 1)
    at = GAIN_AT - (LANES - 128)
    gain = jnp.broadcast_to(gain_ref[...].astype(F32), (8, 128))
    gain = pltpu.roll(gain, (at + 128 - (core * 2 + yl) * 32) & 127, 1)
    tail = jnp.where((lane >= at) & (lane < at + 32), gain, 0.0)
    for s in range(2):
        for j, part in enumerate((high, middle, low)):
            tail = jnp.where(lane == at + 32 + 3 * s + j, part[s : s + 1], tail)
    tail = jnp.concatenate([tail, tail], axis=0).astype(BF)
    rows = pl.ds(begin, 16)
    for i in range(8):
        out_ref[i, :, :UP] = up_ref[rows, :]
        out_ref[i, :, LANES - 128 :] = tail
        out_ref[i, :, UP:GAIN_AT] = down_ref[rows, :]


def packed(place, starts, *arrays):
    arrays = [starts, *arrays]
    return pl.pallas_call(
        pack,
        out_shape=jax.ShapeDtypeStruct((8, 16, LANES), BF),
        in_specs=[pl.BlockSpec(memory_space=pltpu.SMEM)]
        + [pl.BlockSpec(memory_space=pl.ANY)] * 5,
        out_specs=pl.BlockSpec(memory_space=pltpu.VMEM),
        scratch_shapes=[pltpu.SMEM(starts.shape, starts.dtype)]
        + [pltpu.VMEM(v.shape, v.dtype) for v in arrays[1:]]
        + [pltpu.SemaphoreType.DMA((5,))],
        compiler_params=pltpu.CompilerParams(vmem_limit_bytes=4 * 1024 * 1024),
    )(place, *[pltpu.with_memory_space_constraint(v, pltpu.HBM) for v in arrays])


def finish(place_ref, *refs):
    down_ref, up_ref = refs[4:]
    for i in range(4):
        core, yl = (place_ref[3] + i // 2) & 1, (place_ref[1] + i % 2) & 1
        rows = pl.ds(pl.multiple_of(core * 32 + yl * 16, 16), 16)
        up_ref[rows, :] = refs[i][:, :UP]
        down_ref[rows, :] = refs[i][:, UP:GAIN_AT]


def finished(place, *shares_):
    vmem = pl.BlockSpec(memory_space=pltpu.VMEM)
    return pl.pallas_call(
        finish,
        out_shape=[
            jax.ShapeDtypeStruct((ORDER, DOWN), F32),
            jax.ShapeDtypeStruct((ORDER, UP), F32),
        ],
        in_specs=[pl.BlockSpec(memory_space=pltpu.SMEM)] + [vmem] * 4,
        out_specs=[vmem] * 2,
        compiler_params=pltpu.CompilerParams(vmem_limit_bytes=4 * 1024 * 1024),
    )(place, *shares_)


def bring(after_ref, place_ref, *refs):
    sems = refs[6]
    copies = [pltpu.make_async_copy(refs[i], refs[3 + i], sems.at[i]) for i in range(3)]
    for copy in copies:
        copy.start()
    for copy in copies:
        copy.wait()


def brought(after, place, *arrays):
    any_space = pl.BlockSpec(memory_space=pl.ANY)
    size = sum(v.size * 2 for v in arrays)
    return pl.pallas_call(
        bring,
        out_shape=[pltpu.VMEM(v.shape, v.dtype) for v in arrays],
        in_specs=[any_space, pl.BlockSpec(memory_space=pltpu.SMEM)] + [any_space] * 3,
        out_specs=[pl.BlockSpec(memory_space=pltpu.VMEM)] * 3,
        scratch_shapes=[pltpu.SemaphoreType.DMA((3,))],
        compiler_params=pltpu.CompilerParams(vmem_limit_bytes=1024 * 1024),
        cost_estimate=pl.CostEstimate(flops=0, bytes_accessed=2 * size, transcendentals=0),
    )(after, place, *[pltpu.with_memory_space_constraint(v, pltpu.HBM) for v in arrays])


def near_vmem(*arrays):
    return [pltpu.with_memory_space_constraint(v, pltpu.VMEM) for v in arrays]


def shares(place, starts, parts, hidden, frozen, head):
    rows, units = hidden.shape
    width = frozen.shape[1]
    any_space = pl.BlockSpec(memory_space=pl.ANY)
    smem = pl.BlockSpec(memory_space=pltpu.SMEM)
    vmem = pl.BlockSpec(memory_space=pltpu.VMEM)
    *outs, up_rest, grad_low, margin = pl.pallas_call(
        kernel,
        out_shape=[pltpu.VMEM((16 * PLANES, 16, LANES), BF)] * 2
        + [
            pltpu.VMEM((ORDER, width - PLANES * 8 * UP), BF),
            pltpu.VMEM((ORDER, rows), BF),
            jax.ShapeDtypeStruct((8, 128), F32),
        ],
        in_specs=[smem, smem] + [any_space] * 8 + [vmem] * 3,
        out_specs=[vmem] * 5,
        scratch_shapes=[
            pltpu.VMEM((ORDER, units), BF),
            pltpu.VMEM((ORDER, width), BF),
            pltpu.VMEM((4, CHUNKS, 128), F32),
            pltpu.VMEM((CHUNKS, 128), F32),
            pltpu.VMEM((rows, width), F32),
            pltpu.VMEM((256, 16, LANES), BF),
            pltpu.SemaphoreType.DMA((8,)),
        ],
        compiler_params=pltpu.CompilerParams(vmem_limit_bytes=20 * 1024 * 1024),
        cost_estimate=pl.CostEstimate(
            flops=2 * rows * ORDER * (2 * units + 4 * width),
            bytes_accessed=2 * rows * (units + 2 * width) + 4 * 256 * 16 * LANES,
            transcendentals=0,
        ),
    )(place, starts, *parts, *near_vmem(hidden, frozen, head))
    rest = pl.pallas_call(
        second_kernel,
        out_shape=[pltpu.VMEM((16 * (8 - PLANES), 16, LANES), BF)] * 2,
        in_specs=[smem] + [vmem] * 3,
        out_specs=[vmem] * 2,
        scratch_shapes=[pltpu.VMEM((ORDER, (8 - PLANES) * 8 * DOWN // 128 * 128 + 256), BF)],
        compiler_params=pltpu.CompilerParams(vmem_limit_bytes=8 * 1024 * 1024),
        cost_estimate=pl.CostEstimate(
            flops=rows * ORDER * units,
            bytes_accessed=rows * units + 2 * 128 * 16 * LANES,
            transcendentals=0,
        ),
    )(place, *near_vmem(grad_low, up_rest, hidden))
    return outs, rest, margin[0, 0:1]


def device(z, y, x, c):
    return (((z * 2 + y // 2) * 4 + x) * 2 + y % 2) * 2 + c


def ring(values, step, turn=0):
    pairs = []
    for z, y, x, c in itertools.product(range(8), range(4), range(4), range(2)):
        along_y = c ^ turn
        to = device(z, (y + step * along_y) % 4, (x + step * (1 - along_y)) % 4, c)
        pairs.append((device(z, y, x, c), to))
    return lax.ppermute(values, FINE_AXES, pairs)


def other_core(values):
    return lax.ppermute(values, "c", [(0, 1), (1, 0)])


def total_of(*values):
    return sum(v.astype(F32) for v in values)


def local(
    gated_hidden_input,
    frozen,
    head_gradient_rows,
    down_factor_weight,
    up_factor_weight,
    final_norm_gain,
    logratio,
    starts,
):
    yl, core = lax.axis_index("yl"), lax.axis_index("c")
    place = jnp.stack([lax.axis_index("z"), lax.axis_index("yh") * 2 + yl, lax.axis_index("x"), core])

    quarter = packed(
        place,
        starts,
        logratio[0],
        down_factor_weight.T,
        up_factor_weight,
        final_norm_gain[None],
    )
    held = lax.all_to_all(quarter, "z", 0, 0, tiled=True)
    line = jnp.concatenate([held] + [ring(held, step, 1) for step in (1, 2, 3)])
    own = [line] + [ring(line, step) for step in (1, 2, 3)]
    width = frozen.shape[3]
    near = brought(
        line,
        place,
        gated_hidden_input.reshape(-1, gated_hidden_input.shape[3]),
        frozen.reshape(-1, width),
        head_gradient_rows.reshape(-1, width),
    )
    line, *near = lax.optimization_barrier((line, *near))
    other = [other_core(v) for v in (line, *own[1:])]

    first, second, margin = shares(place, starts, [*own, *other], *near)

    lines = []
    for own, other in (first, second):
        came = other_core(other)
        each = own.shape[0] // 4
        chip = [
            total_of(own[each * i : each * i + each], came[each * i : each * i + each]).astype(BF)
            for i in range(4)
        ]
        came = [ring(chip[step], step) for step in (1, 2, 3)]
        lines.append(total_of(chip[0], *came).astype(BF).reshape(4, each // 4, 16, LANES))
    line = jnp.concatenate(lines, axis=1)
    came = [ring(line[step], step, 1) for step in (1, 2, 3)]
    plane = total_of(line[0], *came).astype(BF)
    share = jnp.sum(lax.all_to_all(plane, "z", 0, 0, tiled=True).astype(F32), axis=0)
    spread = [
        lax.ppermute(share, CTX, [(i, i ^ step) for i in range(4)]) for step in (2, 1, 3)
    ]
    down_gradient_t, up_gradient = finished(place, share, *spread)
    return jnp.logaddexp(0.0, -margin), down_gradient_t.T, up_gradient


def solution(mesh):
    fine = Mesh(mesh.devices.reshape(FINE_SHAPE), FINE_AXES)
    return jax.shard_map(
        local,
        mesh=fine,
        in_specs=(
            P(DP, None, CTX, None),
            P(DP, None, CTX, None),
            P(DP, None, CTX, None),
            P(DP, None),
            P(None, DP),
            P(DP),
            P(DP, None, CTX),
            P(DP, None),
        ),
        out_specs=(P(DP), P(DP, None), P(None, DP)),
        check_vma=False,
    )
```

```python
import itertools

import jax
import jax.numpy as jnp
from jax import lax
from jax.experimental import pallas as pl
from jax.experimental.pallas import tpu as pltpu
from jax.sharding import Mesh, PartitionSpec as P

SCALE = 2.0
BETA = 0.1
EPS = 1e-06

FINE_AXES = ("z", "yh", "x", "yl", "c")
FINE_SHAPE = (8, 2, 4, 2, 2)
DP = ("z", "yh", "x")
CTX = ("yl", "c")

LANES = 640
UP = 128
DOWN = 462
GAIN_AT = UP + DOWN
SUMS_AT = GAIN_AT + 32
CHUNKS = 64
ORDER = 64
PLANES = 3
BF, F32 = jnp.bfloat16, jnp.float32
NT = (((1,), (1,)), ((), ()))
NN = (((1,), (0,)), ((), ()))


def dot(a, b, dims):
    return lax.dot_general(a, b, dims, preferred_element_type=F32)


def slots(place, sign, planes):
    py, px, pc = place[1], place[2], place[3]
    dxs = [((sign * (px - x)) & 3) * planes for x in range(4)]
    dys = [((sign * (py - y)) & 3) * planes for y in range(4)]
    for x, yh, other, yl in itertools.product(range(4), range(2), range(2), range(2)):
        dx, dy = dxs[x], dys[yh * 2 + yl]
        yield x, yh, other, yl, jnp.where(pc == other, dx * 4 + dy, dy * 4 + dx)


def to_blocks(place, outs, first, planes, up_share, grad_low, hid, held):
    origin = first * DOWN // 128 * 128
    stop = -(-(first + 8 * planes) * DOWN // 128) * 128
    for begin in range(origin, stop, 1024):
        end = min(begin + 1024, stop)
        held[:, begin - origin : end - origin] = dot(grad_low, hid[:, begin:end], NN).astype(BF)
    for x, yh, other, yl, base in slots(place, -1, planes):
        rows = slice(32 * other + 16 * yl, 32 * other + 16 * yl + 16)
        for z in range(planes):
            chunk = z * 8 + yh * 4 + x
            begin = (first + chunk) * DOWN - origin
            outs[other][base + z, :, :UP] = up_share[rows, chunk * UP : chunk * UP + UP]
            outs[other][base + z, :, UP:GAIN_AT] = held[rows, begin : begin + DOWN]


def kernel(place_ref, starts_ref, *refs):
    parts, (hid, fro, hea) = refs[:8], refs[8:11]
    outs, up_rest, low_ref, margin_ref = refs[11:13], refs[13], refs[14], refs[15]
    wt, up, gains, gain, pol, block, sems = refs[16:]
    width = fro.shape[1]

    loads = [
        pltpu.make_async_copy(parts[i], block.at[pl.ds(32 * i, 32)], sems.at[i]) for i in range(8)
    ]
    for copy in loads:
        copy.start()
    for copy in loads:
        copy.wait()

    pz, py, px, pc = (place_ref[i] for i in range(4))
    sums = jnp.zeros((1, 128), F32)
    for other in range(2):
        for yl in range(2):
            y = (py & 2) + yl
            dy = (py - y) & 3
            inside = jnp.where(pc == other, dy * 8, dy * 32) + pz
            held = block[other * 128 + inside]
            sums += held[0:1, LANES - 128 :].astype(F32)
    lane = SUMS_AT - (LANES - 128)
    sides = [sum(sums[:, lane + 3 * s + j : lane + 3 * s + j + 1] for j in range(3)) for s in (0, 1)]
    margin = BETA * (sides[0] - sides[1])
    margin_ref[...] = jnp.broadcast_to(margin, margin_ref.shape)
    row = lax.broadcasted_iota(jnp.int32, (128, 1), 0)
    position = (row & 63) + ((py & 1) * 2 + pc) * 64
    start = jnp.where(row < 64, starts_ref[0, 0], starts_ref[0, 1])
    weight = jnp.where(row < 64, -BETA, BETA)
    slope = jnp.where(position >= start, weight, 0.0) / (1.0 + jnp.exp(margin))

    for x, yh, other, yl, base in slots(place_ref, 1, 8):
        q = other * 2 + yl
        rows = slice(16 * q, 16 * q + 16)
        for z in range(8):
            chunk = z * 8 + yh * 4 + x
            held = block[other * 128 + base + z]
            up[rows, chunk * UP : (chunk + 1) * UP] = held[:, :UP]
            wt[rows, chunk * DOWN : (chunk + 1) * DOWN] = held[:, UP:GAIN_AT]
            gains[q, chunk : chunk + 1, :] = held[0:1, LANES - 128 :].astype(F32)
    lane = GAIN_AT - (LANES - 128)
    parts_of_gain = [gains[q][:, lane : lane + 32] for q in range(4)]
    ordered = jnp.concatenate(parts_of_gain, axis=1)
    swapped = jnp.concatenate(parts_of_gain[2:] + parts_of_gain[:2], axis=1)
    gain[...] = jnp.where(pc == 0, ordered, swapped)

    tile = 5888
    main = wt.shape[1] // tile
    low = dot(hid[:, main * tile :], wt[:, main * tile :], NT)
    for i in range(main):
        at = slice(i * tile, i * tile + tile)
        low += dot(hid[:, at], wt[:, at], NT)
    low = low.astype(BF)
    low_t = low.astype(F32).T.astype(BF)

    step = 512

    def gained(i):
        pieces = []
        for j in range(step // 128):
            at = slice(i * step + j * 128, i * step + j * 128 + 128)
            chunk = i * (step // 128) + j
            pieces.append(hea[:, at].astype(F32) * gain[chunk : chunk + 1, :])
        return jnp.concatenate(pieces, axis=1)

    def fold(v):
        return sum(v[:, 128 * j : 128 * j + 128] for j in range(step // 128))

    def state_step(i, carry):
        squares, inner = carry
        at = slice(i * step, i * step + step)
        state = fro[:, at].astype(F32) + SCALE * dot(low, up[:, at], NN)
        pol[:, at] = state
        return squares + fold(state * state), inner + fold(gained(i) * state)

    zero = jnp.zeros((128, 128), F32)
    squares, inner = zero, zero
    for i in range(width // step):
        squares, inner = state_step(i, (squares, inner))
    rms = jnp.sqrt(jnp.sum(squares, axis=1, keepdims=True) / width + EPS)
    inner = slope * jnp.sum(inner, axis=1, keepdims=True)
    first = slope / rms
    second = inner / (width * rms * rms * rms)

    packed_here = PLANES * 8 * UP
    total = jnp.zeros((128, ORDER), F32)
    for i in range(width // step):
        at = slice(i * step, (i + 1) * step)
        grad = gained(i) * first - pol[:, at] * second
        high = grad.astype(BF)
        rest = (grad - high.astype(F32)).astype(BF)
        total += dot(high, up[:, at], NT) + dot(rest, up[:, at], NT)
        share = (SCALE * dot(low_t, high, NN)).astype(BF)
        if i * step < packed_here:
            up[:, at] = share
        else:
            up_rest[:, i * step - packed_here : (i + 1) * step - packed_here] = share
    grad_low = (SCALE * total).T.astype(BF)

    low_ref[...] = grad_low
    to_blocks(place_ref, outs, 0, PLANES, up, grad_low, hid, wt)


def second_kernel(place_ref, low_ref, up_rest, hid, *refs):
    to_blocks(
        place_ref, refs[:2], 8 * PLANES, 8 - PLANES, up_rest, low_ref[...], hid, refs[2]
    )


def pack(place_ref, *refs):
    out_ref, sems = refs[5], refs[11]
    copies = [pltpu.make_async_copy(refs[i], refs[6 + i], sems.at[i]) for i in range(5)]
    for copy in copies:
        copy.start()
    for copy in copies:
        copy.wait()
    starts_ref, ratio_ref, down_ref, up_ref, gain_ref = refs[6:11]
    yl, core = place_ref[1] & 1, place_ref[3]
    begin = pl.multiple_of(core * 32 + yl * 16, 16)
    position = lax.broadcasted_iota(jnp.int32, (2, 64), 1) + (yl * 2 + core) * 64
    side = lax.broadcasted_iota(jnp.int32, (2, 64), 0)
    start = jnp.where(side == 0, starts_ref[0, 0], starts_ref[0, 1])
    total = jnp.sum(jnp.where(position >= start, ratio_ref[...], 0.0), axis=1, keepdims=True)
    high = total.astype(BF).astype(F32)
    middle = (total - high).astype(BF).astype(F32)
    low = total - high - middle

    lane = lax.broadcasted_iota(jnp.int32, (8, 128), 1)
    at = GAIN_AT - (LANES - 128)
    gain = jnp.broadcast_to(gain_ref[...].astype(F32), (8, 128))
    gain = pltpu.roll(gain, (at + 128 - (core * 2 + yl) * 32) & 127, 1)
    tail = jnp.where((lane >= at) & (lane < at + 32), gain, 0.0)
    for s in range(2):
        for j, part in enumerate((high, middle, low)):
            tail = jnp.where(lane == at + 32 + 3 * s + j, part[s : s + 1], tail)
    tail = jnp.concatenate([tail, tail], axis=0).astype(BF)
    rows = pl.ds(begin, 16)
    for i in range(8):
        out_ref[i, :, :UP] = up_ref[rows, :]
        out_ref[i, :, LANES - 128 :] = tail
        out_ref[i, :, UP:GAIN_AT] = down_ref[rows, :]


def packed(place, starts, *arrays):
    arrays = [starts, *arrays]
    return pl.pallas_call(
        pack,
        out_shape=jax.ShapeDtypeStruct((8, 16, LANES), BF),
        in_specs=[pl.BlockSpec(memory_space=pltpu.SMEM)]
        + [pl.BlockSpec(memory_space=pl.ANY)] * 5,
        out_specs=pl.BlockSpec(memory_space=pltpu.VMEM),
        scratch_shapes=[pltpu.SMEM(starts.shape, starts.dtype)]
        + [pltpu.VMEM(v.shape, v.dtype) for v in arrays[1:]]
        + [pltpu.SemaphoreType.DMA((5,))],
        compiler_params=pltpu.CompilerParams(vmem_limit_bytes=4 * 1024 * 1024),
    )(place, *[pltpu.with_memory_space_constraint(v, pltpu.HBM) for v in arrays])


def finish(place_ref, *refs):
    down_ref, up_ref = refs[4:]
    for i in range(4):
        core, yl = (place_ref[3] + i // 2) & 1, (place_ref[1] + i % 2) & 1
        rows = pl.ds(pl.multiple_of(core * 32 + yl * 16, 16), 16)
        up_ref[rows, :] = refs[i][:, :UP]
        down_ref[rows, :] = refs[i][:, UP:GAIN_AT]


def finished(place, *shares_):
    vmem = pl.BlockSpec(memory_space=pltpu.VMEM)
    return pl.pallas_call(
        finish,
        out_shape=[
            jax.ShapeDtypeStruct((ORDER, DOWN), F32),
            jax.ShapeDtypeStruct((ORDER, UP), F32),
        ],
        in_specs=[pl.BlockSpec(memory_space=pltpu.SMEM)] + [vmem] * 4,
        out_specs=[vmem] * 2,
        compiler_params=pltpu.CompilerParams(vmem_limit_bytes=4 * 1024 * 1024),
    )(place, *shares_)


def bring(after_ref, place_ref, *refs):
    sems = refs[6]
    copies = [pltpu.make_async_copy(refs[i], refs[3 + i], sems.at[i]) for i in range(3)]
    for copy in copies:
        copy.start()
    for copy in copies:
        copy.wait()


def brought(after, place, *arrays):
    any_space = pl.BlockSpec(memory_space=pl.ANY)
    size = sum(v.size * 2 for v in arrays)
    return pl.pallas_call(
        bring,
        out_shape=[pltpu.VMEM(v.shape, v.dtype) for v in arrays],
        in_specs=[any_space, pl.BlockSpec(memory_space=pltpu.SMEM)] + [any_space] * 3,
        out_specs=[pl.BlockSpec(memory_space=pltpu.VMEM)] * 3,
        scratch_shapes=[pltpu.SemaphoreType.DMA((3,))],
        compiler_params=pltpu.CompilerParams(vmem_limit_bytes=1024 * 1024),
        cost_estimate=pl.CostEstimate(flops=0, bytes_accessed=2 * size, transcendentals=0),
    )(after, place, *[pltpu.with_memory_space_constraint(v, pltpu.HBM) for v in arrays])


def near_vmem(*arrays):
    return [pltpu.with_memory_space_constraint(v, pltpu.VMEM) for v in arrays]


def shares(place, starts, parts, hidden, frozen, head):
    rows, units = hidden.shape
    width = frozen.shape[1]
    any_space = pl.BlockSpec(memory_space=pl.ANY)
    smem = pl.BlockSpec(memory_space=pltpu.SMEM)
    vmem = pl.BlockSpec(memory_space=pltpu.VMEM)
    *outs, up_rest, grad_low, margin = pl.pallas_call(
        kernel,
        out_shape=[pltpu.VMEM((16 * PLANES, 16, LANES), BF)] * 2
        + [
            pltpu.VMEM((ORDER, width - PLANES * 8 * UP), BF),
            pltpu.VMEM((ORDER, rows), BF),
            jax.ShapeDtypeStruct((8, 128), F32),
        ],
        in_specs=[smem, smem] + [any_space] * 8 + [vmem] * 3,
        out_specs=[vmem] * 5,
        scratch_shapes=[
            pltpu.VMEM((ORDER, units), BF),
            pltpu.VMEM((ORDER, width), BF),
            pltpu.VMEM((4, CHUNKS, 128), F32),
            pltpu.VMEM((CHUNKS, 128), F32),
            pltpu.VMEM((rows, width), F32),
            pltpu.VMEM((256, 16, LANES), BF),
            pltpu.SemaphoreType.DMA((8,)),
        ],
        compiler_params=pltpu.CompilerParams(vmem_limit_bytes=20 * 1024 * 1024),
        cost_estimate=pl.CostEstimate(
            flops=2 * rows * ORDER * (2 * units + 4 * width),
            bytes_accessed=2 * rows * (units + 2 * width) + 4 * 256 * 16 * LANES,
            transcendentals=0,
        ),
    )(place, starts, *parts, *near_vmem(hidden, frozen, head))
    rest = pl.pallas_call(
        second_kernel,
        out_shape=[pltpu.VMEM((16 * (8 - PLANES), 16, LANES), BF)] * 2,
        in_specs=[smem] + [vmem] * 3,
        out_specs=[vmem] * 2,
        scratch_shapes=[pltpu.VMEM((ORDER, (8 - PLANES) * 8 * DOWN // 128 * 128 + 256), BF)],
        compiler_params=pltpu.CompilerParams(vmem_limit_bytes=8 * 1024 * 1024),
        cost_estimate=pl.CostEstimate(
            flops=rows * ORDER * units,
            bytes_accessed=rows * units + 2 * 128 * 16 * LANES,
            transcendentals=0,
        ),
    )(place, *near_vmem(grad_low, up_rest, hidden))
    return outs, rest, margin[0, 0:1]


def device(z, y, x, c):
    return (((z * 2 + y // 2) * 4 + x) * 2 + y % 2) * 2 + c


def ring(values, step, turn=0):
    pairs = []
    for z, y, x, c in itertools.product(range(8), range(4), range(4), range(2)):
        along_y = c ^ turn
        to = device(z, (y + step * along_y) % 4, (x + step * (1 - along_y)) % 4, c)
        pairs.append((device(z, y, x, c), to))
    return lax.ppermute(values, FINE_AXES, pairs)


def other_core(values):
    return lax.ppermute(values, "c", [(0, 1), (1, 0)])


def total_of(*values):
    return sum(v.astype(F32) for v in values)


def local(
    gated_hidden_input,
    frozen,
    head_gradient_rows,
    down_factor_weight,
    up_factor_weight,
    final_norm_gain,
    logratio,
    starts,
):
    yl, core = lax.axis_index("yl"), lax.axis_index("c")
    place = jnp.stack([lax.axis_index("z"), lax.axis_index("yh") * 2 + yl, lax.axis_index("x"), core])

    quarter = packed(
        place,
        starts,
        logratio[0],
        down_factor_weight.T,
        up_factor_weight,
        final_norm_gain[None],
    )
    held = lax.all_to_all(quarter, "z", 0, 0, tiled=True)
    line = jnp.concatenate([held] + [ring(held, step, 1) for step in (1, 2, 3)])
    own = [line] + [ring(line, step) for step in (1, 2, 3)]
    width = frozen.shape[3]
    near = brought(
        line,
        place,
        gated_hidden_input.reshape(-1, gated_hidden_input.shape[3]),
        frozen.reshape(-1, width),
        head_gradient_rows.reshape(-1, width),
    )
    line, *near = lax.optimization_barrier((line, *near))
    other = [other_core(v) for v in (line, *own[1:])]

    first, second, margin = shares(place, starts, [*own, *other], *near)

    lines = []
    came_first = other_core(first[1])
    came_first, other = lax.optimization_barrier((came_first, second[1]))
    for own, came in ((first[0], came_first), (second[0], other_core(other))):
        each = own.shape[0] // 4
        chip = [
            total_of(own[each * i : each * i + each], came[each * i : each * i + each]).astype(BF)
            for i in range(4)
        ]
        came = [ring(chip[step], step) for step in (1, 2, 3)]
        lines.append(total_of(chip[0], *came).astype(BF).reshape(4, each // 4, 16, LANES))
    line = jnp.concatenate(lines, axis=1)
    came = [ring(line[step], step, 1) for step in (1, 2, 3)]
    plane = total_of(line[0], *came).astype(BF)
    share = jnp.sum(lax.all_to_all(plane, "z", 0, 0, tiled=True).astype(F32), axis=0)
    spread = [
        lax.ppermute(share, CTX, [(i, i ^ step) for i in range(4)]) for step in (2, 1, 3)
    ]
    down_gradient_t, up_gradient = finished(place, share, *spread)
    return jnp.logaddexp(0.0, -margin), down_gradient_t.T, up_gradient


def solution(mesh):
    fine = Mesh(mesh.devices.reshape(FINE_SHAPE), FINE_AXES)
    return jax.shard_map(
        local,
        mesh=fine,
        in_specs=(
            P(DP, None, CTX, None),
            P(DP, None, CTX, None),
            P(DP, None, CTX, None),
            P(DP, None),
            P(None, DP),
            P(DP),
            P(DP, None, CTX),
            P(DP, None),
        ),
        out_specs=(P(DP), P(DP, None), P(None, DP)),
        check_vma=False,
    )
```
